32 devices in a mesh: gx: 8 (over y, x, core), gy: 4 (over z).
Axes of the slice: x: 2, y: 2, z: 4, core: 2. Of those that a mesh axis runs over, the one named last changes fastest.
Arguments:
- stratum_warmth_celsius: float32 [50, 512, 512], P(None, 'gx', 'gy'), may hold values from -6 to 2
- stratum_mass_per_volume: float32 [50, 512, 512], P(None, 'gx', 'gy'), may hold values from 0.1 to 0.55
- stratum_melt_fluid: float32 [50, 512, 512], P(None, 'gx', 'gy'), may hold values from 0 to 0.04
- stratum_crystal_size: float32 [50, 512, 512], P(None, 'gx', 'gy'), may hold values from 0.2 to 2
- pile_stratum_tally: int32 [512, 512], P('gx', 'gy'), may hold values from 1 to 50, as said below
- pile_atmospheric_warmth: float32 [512, 512], P('gx', 'gy'), may hold values from -6 to 6
- topmost_thermal_factor: float32 [512, 512], P('gx', 'gy'), may hold values from 0.5 to 5
- movable_topmost_powder: float32 [512, 512], P('gx', 'gy'), may hold values from 0 to 1
- first_axis_gust_fraction: float32 [512, 512], P('gx', 'gy'), may hold values from -0.3 to 0.3
- second_axis_gust_fraction: float32 [512, 512], P('gx', 'gy'), may hold values from -0.3 to 0.3
- extra_stratum_warmth: float32 [50, 3072], P(None, ('gx', 'gy')), may hold values from -4 to 0
- extra_stratum_mass_per_volume: float32 [50, 3072], P(None, ('gx', 'gy')), may hold values from 0.4 to 0.8
- parent_pile: int32 [3072], P(('gx', 'gy')), may hold values from 0 to 262143, as said below
- pile_stream_segment: int32 [512, 512], P('gx', 'gy'), may hold values from 0 to 8191, as said below
- segment_result_index: int32 [131072], replicated, may hold values from 0 to 131071, as said below
Outputs:
- drift_final: float32 [512, 512], P('gx', 'gy')
- fresh_warmth: float32 [50, 512, 512], P(None, 'gx', 'gy')
- retained_fluid: float32 [50, 512, 512], P(None, 'gx', 'gy')
- extra_stratum_fresh_warmth: float32 [50, 3072], P(None, ('gx', 'gy'))
- segment_thaw_arrival: float32 [131072], P(('gx', 'gy'))
The draws below stay inside these ranges and needn't reach their ends.
Inputs may be any that keep to these rules, and one draw needn't show every extreme that they name: `pile_stratum_tally`: columns named by parent_pile have 50 layers. `parent_pile`: no column is named twice. Of the 96 slots of one device at most 8 name columns of one tile, and one tile is named 8 times by the slots of every device. `pile_stream_segment`: codes of 4096 or more occur only in tiles with a + 1 < 8. segment_result_index is a permutation. Of the 4096 reaches t * 4096 to (t + 1) * 4096 - 1 of any tile t, exactly 128 have slots in each block h * 4096 to (h + 1) * 4096 - 1.
All inputs are finite; a program needn't handle non-finite values.
Results may differ from the reference program's by a relative error of at most 0.00002.
Values sent between devices are 32-bit elements; how exact they have to be, the bound alone decides.
A program may use at most 64 MiB of HBM per device.

```python
import math
import jax
import jax.numpy as jnp
from jax import lax

TX = 64
TY = 128
PACK_STRATA = 50
EXTRA_STRATA = 50
STEPS = 4
PAIR = 8
R_DEV = 4096
GRID_EXTENT_FIRST = 512
GRID_EXTENT_OTHER = 512
THICK_PILE_TOTAL = 3072
NREACH = 131072


def deep_layout(key):
    tiles_x = GRID_EXTENT_FIRST // TX
    tiles_y = GRID_EXTENT_OTHER // TY
    ndevices = tiles_x * tiles_y
    columns = TX * TY
    slots = PAIR * 3 // 8 * ndevices
    k_rank, k_pick, k_score, k_shuffle, k_offset, k_colperm = jax.random.split(key, 6)
    ranking = jax.random.permutation(k_rank, ndevices)
    weight = jnp.where(ranking < ndevices // 4, PAIR, PAIR // 4)
    favoured = jnp.argsort(ranking, stable=True)[jax.random.randint(k_pick, (), 0, ndevices // 4)]
    entry = jnp.arange(ndevices * PAIR, dtype=jnp.int32)
    entry_owner = entry // PAIR
    entry_copy = entry % PAIR
    admissible = entry_copy < weight[entry_owner]
    score = jax.random.randint(k_score, (ndevices, ndevices * PAIR), 0, 2 ** 16) * (ndevices * PAIR) + entry[None, :]
    score = jnp.where((entry_owner == favoured)[None, :], score - 2 ** 28, score)
    score = jnp.where(admissible[None, :], score, score + 2 ** 29)
    order = jnp.argsort(score, axis=1, stable=True)[:, :slots]
    owners = entry_owner[order]
    shuffles = jax.vmap(lambda sub: jax.random.permutation(sub, slots))(jax.random.split(k_shuffle, ndevices))
    owners = jnp.take_along_axis(owners, shuffles, axis=1)
    flat = owners.reshape(-1)
    sorted_index = jnp.argsort(flat, stable=True)
    counts = jax.ops.segment_sum(jnp.ones_like(flat), flat, ndevices)
    starts = jnp.cumsum(counts) - counts
    within = jnp.arange(flat.shape[0], dtype=jnp.int32) - starts[flat[sorted_index]]
    rank_in = jnp.zeros_like(flat).at[sorted_index].set(within)
    offset = jax.random.randint(k_offset, (ndevices,), 0, columns)
    colperm = jax.random.permutation(k_colperm, columns)
    local = colperm[(rank_in + offset[flat]) % columns]
    return (flat * columns + local).astype(jnp.int32)


def draw_parent_pile(key, part):
    return deep_layout(key)


def draw_pile_stratum_tally(key, part):
    layout = deep_layout(key)
    key = jax.random.fold_in(key, 11)
    tiles_y = GRID_EXTENT_OTHER // TY
    columns = TX * TY
    counts = jax.random.randint(key, (GRID_EXTENT_FIRST, GRID_EXTENT_OTHER), 1, PACK_STRATA + 1)
    owner = layout // columns
    local = layout % columns
    first_axis_index = owner // tiles_y * TX + local // TY
    second_axis_index = owner % tiles_y * TY + local % TY
    marked = jnp.zeros((GRID_EXTENT_FIRST, GRID_EXTENT_OTHER), jnp.int32).at[first_axis_index, second_axis_index].set(1)
    return jnp.where(marked == 1, PACK_STRATA, counts).astype(jnp.int32)


def draw_pile_stream_segment(key, part):
    key = jax.random.fold_in(key, 23)
    k_east, k_pick = jax.random.split(key)
    tiles_x = GRID_EXTENT_FIRST // TX
    tile_a = (jnp.arange(GRID_EXTENT_FIRST, dtype=jnp.int32) // TX)[:, None]
    eastward = (jax.random.randint(k_east, (GRID_EXTENT_FIRST, GRID_EXTENT_OTHER), 0, 4) == 0) & (tile_a + 1 < tiles_x)
    return (eastward.astype(jnp.int32) * R_DEV + jax.random.randint(k_pick, (GRID_EXTENT_FIRST, GRID_EXTENT_OTHER), 0, R_DEV)).astype(jnp.int32)


def draw_segment_result_index(key, part):
    key = jax.random.fold_in(key, 37)
    ndevices = GRID_EXTENT_FIRST // TX * (GRID_EXTENT_OTHER // TY)
    per_peer = R_DEV // ndevices
    k_local, k_holder = jax.random.split(key)
    local_perm = jax.vmap(lambda sub: jax.random.permutation(sub, R_DEV))(jax.random.split(k_local, ndevices)).astype(jnp.int32)
    holder = local_perm // per_peer
    within = local_perm % per_peer
    tile = jnp.arange(ndevices, dtype=jnp.int32)[:, None]
    incoming = tile * per_peer + within
    holder_perm = jax.vmap(lambda sub: jax.random.permutation(sub, R_DEV))(jax.random.split(k_holder, ndevices)).astype(jnp.int32)
    position = holder_perm[holder, incoming]
    return (holder * R_DEV + position).reshape(-1).astype(jnp.int32)


def level_of(stream_key, dims, cuts, smallest, largest):
    loudness = 1.0
    for dim, blocks in cuts:
        steps = jax.random.uniform(jax.random.fold_in(jax.random.fold_in(stream_key, 6), dim), (blocks,), jnp.float32, smallest / len(cuts), largest / len(cuts))
        loudness = loudness * jnp.repeat(jnp.exp(steps), dims[dim] // blocks).reshape((-1,) + (1,) * (len(dims) - 1 - dim))
    return loudness


def setup_inputs(seed: int = 0) -> dict:
    streams_of = jax.random.split(jax.random.key(seed), 16)
    return {
        "stratum_warmth_celsius": jnp.clip(-6.0 + 8.0 * jax.random.uniform(streams_of[0], (PACK_STRATA, GRID_EXTENT_FIRST, GRID_EXTENT_OTHER), jnp.float32) ** level_of(streams_of[0], (PACK_STRATA, GRID_EXTENT_FIRST, GRID_EXTENT_OTHER), ((1, 8), (2, 4)), -0.2, 0.2), -6.0, 2.0),
        "stratum_mass_per_volume": jnp.clip(0.1 + 0.45000001 * jax.random.uniform(streams_of[1], (PACK_STRATA, GRID_EXTENT_FIRST, GRID_EXTENT_OTHER), jnp.float32) ** level_of(streams_of[1], (PACK_STRATA, GRID_EXTENT_FIRST, GRID_EXTENT_OTHER), ((1, 8), (2, 4)), -0.2, 0.2), 0.1, 0.55),
        "stratum_melt_fluid": jnp.clip(0.04 * jax.random.uniform(streams_of[2], (PACK_STRATA, GRID_EXTENT_FIRST, GRID_EXTENT_OTHER), jnp.float32) ** level_of(streams_of[2], (PACK_STRATA, GRID_EXTENT_FIRST, GRID_EXTENT_OTHER), ((1, 8), (2, 4)), -0.2, 0.2), 0.0, 0.04),
        "stratum_crystal_size": jnp.clip(jnp.exp(math.log(2.0) - 2.3025851 * jax.random.uniform(streams_of[3], (PACK_STRATA, GRID_EXTENT_FIRST, GRID_EXTENT_OTHER), jnp.float32) ** level_of(streams_of[3], (PACK_STRATA, GRID_EXTENT_FIRST, GRID_EXTENT_OTHER), ((1, 8), (2, 4)), -0.2, 0.2)), 0.2, 2.0),
        "pile_stratum_tally": draw_pile_stratum_tally(jax.random.fold_in(streams_of[15], 71), 0),
        "pile_atmospheric_warmth": jnp.clip(jax.random.uniform(streams_of[5], (GRID_EXTENT_FIRST, GRID_EXTENT_OTHER), jnp.float32, -6.0, 6.0) * level_of(streams_of[5], (GRID_EXTENT_FIRST, GRID_EXTENT_OTHER), ((0, 8), (1, 4)), -0.4, 0.0), -6.0, 6.0),
        "topmost_thermal_factor": jnp.clip(jnp.exp(math.log(5.0) - 2.3025851 * jax.random.uniform(streams_of[6], (GRID_EXTENT_FIRST, GRID_EXTENT_OTHER), jnp.float32) ** level_of(streams_of[6], (GRID_EXTENT_FIRST, GRID_EXTENT_OTHER), ((0, 8), (1, 4)), -0.2, 0.2)), 0.5, 5.0),
        "movable_topmost_powder": jnp.clip(1.0 * jax.random.uniform(streams_of[7], (GRID_EXTENT_FIRST, GRID_EXTENT_OTHER), jnp.float32) ** level_of(streams_of[7], (GRID_EXTENT_FIRST, GRID_EXTENT_OTHER), ((0, 8), (1, 4)), -0.2, 0.2), 0.0, 1.0),
        "first_axis_gust_fraction": jnp.clip(jax.random.uniform(streams_of[8], (GRID_EXTENT_FIRST, GRID_EXTENT_OTHER), jnp.float32, -0.3, 0.3) * level_of(streams_of[8], (GRID_EXTENT_FIRST, GRID_EXTENT_OTHER), ((0, 8), (1, 4)), -0.4, 0.0), -0.3, 0.3),
        "second_axis_gust_fraction": jnp.clip(jax.random.uniform(streams_of[9], (GRID_EXTENT_FIRST, GRID_EXTENT_OTHER), jnp.float32, -0.3, 0.3) * level_of(streams_of[9], (GRID_EXTENT_FIRST, GRID_EXTENT_OTHER), ((0, 8), (1, 4)), -0.4, 0.0), -0.3, 0.3),
        "extra_stratum_warmth": jnp.clip(-4.0 + 4.0 * jax.random.uniform(streams_of[10], (EXTRA_STRATA, THICK_PILE_TOTAL), jnp.float32) ** level_of(streams_of[10], (EXTRA_STRATA, THICK_PILE_TOTAL), ((1, 32),), -0.2, 0.2), -4.0, 0.0),
        "extra_stratum_mass_per_volume": jnp.clip(0.4 + 0.4 * jax.random.uniform(streams_of[11], (EXTRA_STRATA, THICK_PILE_TOTAL), jnp.float32) ** level_of(streams_of[11], (EXTRA_STRATA, THICK_PILE_TOTAL), ((1, 32),), -0.2, 0.2), 0.4, 0.8),
        "parent_pile": draw_parent_pile(jax.random.fold_in(streams_of[15], 71), 0),
        "pile_stream_segment": draw_pile_stream_segment(jax.random.fold_in(streams_of[15], 71), 0),
        "segment_result_index": draw_segment_result_index(jax.random.fold_in(streams_of[15], 71), 0),
    }


diffusion_number = 0.1
melt_rate = 0.02
holding_rate = 0.03


def advance(padded, east_speed, north_speed):
    centre = padded[1:-1, 1:-1]
    before_x = padded[:-2, 1:-1]
    after_x = padded[2:, 1:-1]
    before_y = padded[1:-1, :-2]
    after_y = padded[1:-1, 2:]
    change = -jnp.maximum(east_speed, 0.0) * (centre - before_x) - jnp.minimum(east_speed, 0.0) * (after_x - centre)
    change = change - jnp.maximum(north_speed, 0.0) * (centre - before_y) - jnp.minimum(north_speed, 0.0) * (after_y - centre)
    return centre + change + diffusion_number * (before_x + after_x + before_y + after_y - 4.0 * centre)


def thomas(diag, rhs, link_up, link_down):
    def forward(carry, inputs):
        ratio_prev, value_prev = carry
        diag_row, rhs_row, up_row, down_row = inputs
        denom = diag_row - up_row * ratio_prev
        value = (rhs_row + up_row * value_prev) / denom
        ratio = down_row / denom
        return (ratio, value), (ratio, value)

    zero_row = jnp.zeros_like(diag[0])
    unused, (ratios, values) = lax.scan(forward, (zero_row, zero_row), (diag, rhs, link_up, link_down))

    def backward(below, inputs):
        ratio, value = inputs
        result = value + ratio * below
        return result, result

    unused, solved = lax.scan(backward, zero_row, (ratios, values), reverse=True)
    return solved


def pile_thermal_tridiag_pass(start_temp, thermal_diffusivity, count, thermal_flux_between, air, pivot_entries, forcing_vector, thick_flagging):
    layer = lax.broadcasted_iota(jnp.int32, start_temp.shape, 0)
    live_next = (layer + 1 < count[None]).astype(thermal_diffusivity.dtype)
    link = 0.5 * (thermal_diffusivity[:-1] + thermal_diffusivity[1:]) * live_next[:-1]
    zero_layer = jnp.zeros_like(thermal_diffusivity[:1])
    link_up = jnp.concatenate([zero_layer, link], axis=0)
    link_down = jnp.concatenate([link, zero_layer], axis=0)
    ground = thermal_diffusivity * (layer == count[None] - 1).astype(thermal_diffusivity.dtype)
    surface = jnp.concatenate([thermal_flux_between[None], jnp.zeros_like(thermal_diffusivity[1:])], axis=0)
    basal_stratum = thermal_diffusivity[-1]
    lowest = thick_flagging * basal_stratum * basal_stratum / (pivot_entries + basal_stratum)
    gained = thick_flagging * basal_stratum * forcing_vector / (pivot_entries + basal_stratum)
    lowest_full = jnp.concatenate([jnp.zeros_like(thermal_diffusivity[:-1]), lowest[None]], axis=0)
    gained_full = jnp.concatenate([jnp.zeros_like(thermal_diffusivity[:-1]), gained[None]], axis=0)
    diag = 1.0 + link_up + link_down + ground + surface - lowest_full
    rhs = start_temp + surface * air[None] + gained_full
    return thomas(diag, rhs, link_up, link_down)


def packed_piles(deep_temp, deep_rho):
    kdeep = 1.0 + 24.0 * deep_rho * deep_rho
    elink = 0.5 * (kdeep[:-1] + kdeep[1:])
    zero_layer = jnp.zeros_like(kdeep[:1])
    link_up = jnp.concatenate([zero_layer, elink], axis=0)
    link_down = jnp.concatenate([elink, zero_layer], axis=0)
    ground = jnp.concatenate([jnp.zeros_like(kdeep[:-1]), kdeep[-1:]], axis=0)
    diag = 1.0 + link_up + link_down + ground

    def upward(carry, inputs):
        diag_next, rhs_next = carry
        diag_row, rhs_row, down_row = inputs
        eliminated_forcing = diag_row - down_row * down_row / diag_next
        eliminated_superdiag = rhs_row + down_row * rhs_next / diag_next
        return (eliminated_forcing, eliminated_superdiag), (eliminated_forcing, eliminated_superdiag)

    start = (jnp.ones_like(kdeep[0]), jnp.zeros_like(kdeep[0]))
    unused, (eliminated_forcing, eliminated_superdiag) = lax.scan(upward, start, (diag, deep_temp, link_down), reverse=True)
    return eliminated_forcing, eliminated_superdiag, link_up


def back_substitute(first, eliminated_forcing, eliminated_superdiag, link_up):
    def downward(above, inputs):
        dprime_row, rprime_row, up_row = inputs
        value = (rprime_row + up_row * above) / dprime_row
        return value, value

    unused, rest = lax.scan(downward, first, (eliminated_forcing[1:], eliminated_superdiag[1:], link_up[1:]))
    return jnp.concatenate([first[None], rest], axis=0)


def fluid_seepage(new_temp, density, liquid, count):
    layer = lax.broadcasted_iota(jnp.int32, new_temp.shape, 0)
    live = (layer < count[None]).astype(new_temp.dtype)
    melt = melt_rate * jnp.maximum(new_temp, 0.0)
    holding = holding_rate * (1.0 - density)

    def downward(flux, inputs):
        live_row, water_row, melt_row, hold_row = inputs
        avail = live_row * (water_row + melt_row) + flux
        kept = live_row * jnp.minimum(avail, hold_row)
        return avail - kept, kept

    stream_discharge, kept = lax.scan(downward, jnp.zeros_like(new_temp[0]), (live, liquid, melt, holding))
    return kept, stream_discharge


def reference(stratum_warmth_celsius, stratum_mass_per_volume, stratum_melt_fluid, stratum_crystal_size, pile_stratum_tally, pile_atmospheric_warmth, topmost_thermal_factor, movable_topmost_powder, first_axis_gust_fraction, second_axis_gust_fraction, extra_stratum_warmth, extra_stratum_mass_per_volume, parent_pile, pile_stream_segment, segment_result_index):
    gust_drifting = movable_topmost_powder
    for step in range(STEPS):
        gust_drifting = advance(jnp.pad(gust_drifting, 1), first_axis_gust_fraction, second_axis_gust_fraction)
    thermal_flux_between = topmost_thermal_factor / (1.0 + gust_drifting)
    thermal_diffusivity = 1.0 + 24.0 * stratum_mass_per_volume * stratum_mass_per_volume * stratum_crystal_size
    eliminated_forcing, eliminated_superdiag, interface_coupling = packed_piles(extra_stratum_warmth, extra_stratum_mass_per_volume)
    columns = TX * TY
    tiles_y = GRID_EXTENT_OTHER // TY
    owner = parent_pile // columns
    local = parent_pile % columns
    first_axis_index = (owner // tiles_y) * TX + local // TY
    second_axis_index = (owner % tiles_y) * TY + local % TY
    pivot_entries = jnp.zeros((GRID_EXTENT_FIRST, GRID_EXTENT_OTHER), jnp.float32).at[first_axis_index, second_axis_index].set(eliminated_forcing[0])
    forcing_vector = jnp.zeros((GRID_EXTENT_FIRST, GRID_EXTENT_OTHER), jnp.float32).at[first_axis_index, second_axis_index].set(eliminated_superdiag[0])
    thick_flagging = jnp.zeros((GRID_EXTENT_FIRST, GRID_EXTENT_OTHER), jnp.float32).at[first_axis_index, second_axis_index].set(jnp.ones_like(eliminated_forcing[0]))
    fresh_warmth = pile_thermal_tridiag_pass(stratum_warmth_celsius, thermal_diffusivity, pile_stratum_tally, thermal_flux_between, pile_atmospheric_warmth, pivot_entries, forcing_vector, thick_flagging)
    basal_stratum = thermal_diffusivity[-1][first_axis_index, second_axis_index]
    topmost_into_extra = (eliminated_superdiag[0] + basal_stratum * fresh_warmth[-1][first_axis_index, second_axis_index]) / (eliminated_forcing[0] + basal_stratum)
    extra_stratum_fresh_warmth = back_substitute(topmost_into_extra, eliminated_forcing, eliminated_superdiag, interface_coupling)
    retained_fluid, stream_discharge = fluid_seepage(fresh_warmth, stratum_mass_per_volume, stratum_melt_fluid, pile_stratum_tally)
    tile_a = (jnp.arange(GRID_EXTENT_FIRST, dtype=jnp.int32) // TX)[:, None]
    tile_b = (jnp.arange(GRID_EXTENT_OTHER, dtype=jnp.int32) // TY)[None, :]
    eastward = (pile_stream_segment >= R_DEV).astype(jnp.int32)
    reach = ((tile_a + eastward) * tiles_y + tile_b) * R_DEV + pile_stream_segment % R_DEV
    slots = segment_result_index[reach]
    segment_thaw_arrival = jnp.zeros((NREACH,), jnp.float32).at[slots.reshape(-1)].add(stream_discharge.reshape(-1))
    return gust_drifting, fresh_warmth, retained_fluid, extra_stratum_fresh_warmth, segment_thaw_arrival
```

```python
import functools

import jax
import jax.numpy as jnp
from jax import lax
from jax.experimental import pallas as pl
from jax.experimental.pallas import tpu as pltpu
from jax.sharding import PartitionSpec as P

STEPS = 4
PAIR = 8
LANES = 128

diffusion_number = 0.1
melt_rate = 0.02
holding_rate = 0.03

HIGH = lax.Precision.HIGHEST
NT = (((1,), (1,)), ((), ()))
TN = (((0,), (0,)), ((), ()))
NN = (((1,), (0,)), ((), ()))


def quotient(x, size):
    if size & (size - 1) == 0:
        return lax.shift_right_logical(x, jnp.full_like(x, size.bit_length() - 1))
    return lax.div(x, jnp.full_like(x, size))


def remainder(x, size):
    if size & (size - 1) == 0:
        return x & (size - 1)
    return lax.rem(x, jnp.full_like(x, size))


def rows_of(shape):
    return lax.broadcasted_iota(jnp.int32, shape, 0)


def lanes_of(shape):
    return lax.broadcasted_iota(jnp.int32, shape, 1)


def dot(a, b, dims, precision=None):
    return lax.dot_general(a, b, dims, precision=precision, preferred_element_type=jnp.float32)


def lane_chunk(i):
    return pl.ds(pl.multiple_of(i * LANES, LANES), LANES)


def fill_places(out_ref, index_ref, places, rows, unroll=4):
    def body(i, carry):
        hit = rows_of((places, LANES)) == index_ref[pl.ds(i, 1), :]
        out_ref[0:places, lane_chunk(i)] = jnp.where(hit, 1.0, 0.0).astype(jnp.bfloat16)
        return carry

    lax.fori_loop(0, rows, body, 0, unroll=unroll)


def fill_values(out_ref, index_ref, part_refs, places, rows, unroll=4):
    def body(i, carry):
        hit = rows_of((places, LANES)) == index_ref[pl.ds(i, 1), :]
        for p, part_ref in enumerate(part_refs):
            out_ref[p * places : (p + 1) * places, lane_chunk(i)] = jnp.where(
                hit, part_ref[pl.ds(i, 1), :], 0.0
            ).astype(jnp.bfloat16)
        return carry

    lax.fori_loop(0, rows, body, 0, unroll=unroll)


def split_three(value, part_refs):
    first = value.astype(jnp.bfloat16).astype(jnp.float32)
    second = (value - first).astype(jnp.bfloat16).astype(jnp.float32)
    part_refs[0][...] = first
    part_refs[1][...] = second
    part_refs[2][...] = value - first - second


def placed_sum(a_ref, b_ref, places, lanes, width, parts):
    both = dot(a_ref[0 : parts * places, 0:width], b_ref[0:lanes, 0:width], NT)
    return [both[p * places : (p + 1) * places] for p in range(parts)]


def deep_eliminate(temp_ref, rho_ref, elink_ref, dprime_ref, rprime_ref):
    layers = temp_ref.shape[0]
    kdeep = 1.0 + 24.0 * rho_ref[...] * rho_ref[...]
    elink_ref[0 : layers - 1, :] = 0.5 * (kdeep[:-1] + kdeep[1:])
    elink_ref[layers - 1 : layers, :] = jnp.zeros_like(kdeep[:1])
    elink = elink_ref[...]
    dprime_ref[...] = 1.0 + elink
    dprime_ref[1:layers, :] = dprime_ref[1:layers, :] + elink[:-1]
    last = pl.ds(layers - 1, 1)
    diag = dprime_ref[last, :] + kdeep[layers - 1 :]
    rhs = temp_ref[last, :]
    dprime_ref[last, :] = diag
    rprime_ref[last, :] = rhs

    def body(step, carry):
        diag, rhs = carry
        row = pl.ds(layers - 2 - step, 1)
        link = elink_ref[row, :]
        ratio = link / diag
        diag = dprime_ref[row, :] - link * ratio
        rhs = temp_ref[row, :] + ratio * rhs
        dprime_ref[row, :] = diag
        rprime_ref[row, :] = rhs
        return diag, rhs

    return lax.fori_loop(0, layers - 1, body, (diag, rhs), unroll=7)


def deep_positions(pile_row, pile_col, columns):
    slots = pile_row.shape[1]
    owner_row = quotient(pile_row, columns)
    owner_col = quotient(pile_col, columns)
    square = (slots, slots)
    earlier = (owner_row == owner_col) & (lanes_of(square) < rows_of(square))
    position = jnp.sum(jnp.where(earlier, 1.0, 0.0), axis=1, keepdims=True).astype(jnp.int32)
    return owner_row, owner_col, position


def as_column(row):
    size = row.shape[1]
    eye = rows_of((size, size)) == lanes_of((size, size))
    return jnp.sum(jnp.where(eye, row, 0.0), axis=1, keepdims=True)


def as_row(column):
    size = column.shape[0]
    eye = rows_of((size, size)) == lanes_of((size, size))
    return jnp.sum(jnp.where(eye, column, 0.0), axis=0, keepdims=True)


def deep_message(diag, rhs, pile_row, pile_col, columns, devices):
    owner_row, owner_col, position = deep_positions(pile_row, pile_col, columns)
    slots = pile_row.shape[1]
    lane = lanes_of((slots, LANES))
    cell = (remainder(pile_col, columns) + 1).astype(jnp.float32)
    table = jnp.where(lane == position, as_column(diag), 0.0)
    table = jnp.where(lane == position + PAIR, as_column(rhs), table)
    table = jnp.where(lane == position + 2 * PAIR, cell, table)
    pick = jnp.where(rows_of((devices, slots)) == owner_row, 1.0, 0.0)
    return dot(pick, table, NN, HIGH)


def ranks(holder_ref, rank_ref, hit_ref, count_ref, devices, rows):
    def fill(i, carry):
        hit = rows_of((devices, LANES)) == holder_ref[pl.ds(i, 1), :]
        place = pl.ds(pl.multiple_of(i * devices, devices), devices)
        hit_ref[place, :] = jnp.where(hit, 1.0, 0.0).astype(jnp.bfloat16)
        return carry

    lax.fori_loop(0, rows, fill, 0, unroll=4)
    shape = (LANES, 2 * LANES)
    before = (rows_of(shape) < lanes_of(shape)) | (lanes_of(shape) >= LANES)
    count_ref[...] = dot(hit_ref[...], jnp.where(before, 1.0, 0.0).astype(jnp.bfloat16), NN)

    def number(i, base):
        hit = rows_of((devices, LANES)) == holder_ref[pl.ds(i, 1), :]
        place = pl.ds(pl.multiple_of(i * devices, devices), devices)
        count = count_ref[place, 0:LANES] + base
        rank_ref[pl.ds(i, 1), :] = jnp.sum(
            jnp.where(hit, count, 0.0), axis=0, keepdims=True
        ).astype(jnp.int32)
        return base + count_ref[place, LANES : 2 * LANES]

    lax.fori_loop(0, rows, number, jnp.zeros((devices, LANES), jnp.float32), unroll=4)


def drift(snow, east, north, tile_x, tile_y, first_x, first_y, extent_x, extent_y, halo):
    shape = snow.shape
    x = rows_of(shape)
    y = lanes_of(shape)
    x = first_x + jnp.where(x >= tile_x + halo, x - shape[0], x)
    y = first_y + jnp.where(y >= tile_y + halo, y - shape[1], y)
    inside = (x >= 0) & (x < extent_x) & (y >= 0) & (y < extent_y)
    east_up, east_down = jnp.maximum(east, 0.0), jnp.minimum(east, 0.0)
    north_up, north_down = jnp.maximum(north, 0.0), jnp.minimum(north, 0.0)
    for step in range(STEPS):
        before_x = pltpu.roll(snow, 1, 0)
        after_x = pltpu.roll(snow, shape[0] - 1, 0)
        before_y = pltpu.roll(snow, 1, 1)
        after_y = pltpu.roll(snow, shape[1] - 1, 1)
        change = -east_up * (snow - before_x) - east_down * (after_x - snow)
        change = change - north_up * (snow - before_y) - north_down * (after_y - snow)
        snow = (
            snow
            + change
            + diffusion_number * (before_x + after_x + before_y + after_y - 4.0 * snow)
        )
        snow = jnp.where(inside, snow, 0.0)
    return snow[0:tile_x, 0:tile_y]


def deep_places(got, tile_x, tile_y):
    devices = got.shape[0]
    highs, lows, diags, rhss = [], [], [], []
    for k in range(PAIR):
        cell = got[:, 2 * PAIR + k : 2 * PAIR + k + 1].astype(jnp.int32) - 1
        full = cell >= 0
        cell = jnp.maximum(cell, 0)
        high = (lanes_of((devices, tile_x)) == quotient(cell, tile_y)) & full
        low = (lanes_of((devices, tile_y)) == remainder(cell, tile_y)) & full
        highs.append(jnp.where(high, 1.0, 0.0))
        low = jnp.where(low, 1.0, 0.0)
        lows.append(low)
        diags.append(low * got[:, k : k + 1])
        rhss.append(low * got[:, PAIR + k : PAIR + k + 1])
    high = jnp.concatenate(highs, axis=0)
    low = jnp.concatenate(lows, axis=0)
    table = jnp.concatenate(
        [jnp.concatenate(diags, axis=0), jnp.concatenate(rhss, axis=0), low], axis=1
    )
    dense = dot(high, table, TN, HIGH)
    return (
        high,
        low,
        dense[:, 0:tile_y],
        dense[:, tile_y : 2 * tile_y],
        dense[:, 2 * tile_y :],
    )


def deep_answers(high, low, dense, devices):
    found = dot(high, dense, NN, HIGH) * low
    lane = lanes_of((devices, LANES))
    answer = jnp.zeros((devices, LANES), jnp.float32)
    for k in range(PAIR):
        value = jnp.sum(found[k * devices : (k + 1) * devices], axis=1, keepdims=True)
        answer = jnp.where(lane == k, value, answer)
    return answer


def eliminate(temp_ref, rho_ref, size_ref, tally, exchange, air, ratio_ref, value_ref):
    layers = temp_ref.shape[0]

    def kappa_of(i):
        rho = rho_ref[i]
        return 1.0 + 24.0 * rho * rho * size_ref[i]

    def row(i, kappa, up, ratio, value, diag_more, rhs_more):
        kappa_next = kappa_of(i + 1)
        down = jnp.where(i + 1 < tally, 0.5 * (kappa + kappa_next), 0.0)
        diag = 1.0 + up + down + jnp.where(i == tally - 1, kappa, 0.0)
        rhs = temp_ref[i]
        if diag_more is not None:
            diag = diag + diag_more
            rhs = rhs + rhs_more
        inverse = 1.0 / (diag - up * ratio)
        value = (rhs + up * value) * inverse
        ratio = down * inverse
        ratio_ref[i] = ratio
        value_ref[i] = value
        return kappa_next, down, ratio, value

    zero = jnp.zeros_like(air)
    carry = row(0, kappa_of(0), zero, zero, zero, exchange, exchange * air)
    return lax.fori_loop(
        1, layers - 1, lambda i, c: row(i, *c, None, None), carry, unroll=2
    )


def bottom_row(temp_ref, tally, carry, base_diag, base_rhs, flag):
    layers = temp_ref.shape[0]
    kappa, up, ratio, value = carry
    scale = flag * kappa / (base_diag + kappa)
    diag = 1.0 + up + jnp.where(tally == layers, kappa, 0.0) - scale * kappa
    rhs = temp_ref[layers - 1] + scale * base_rhs
    bottom = (rhs + up * value) / (diag - up * ratio)
    surface_deep = (base_rhs + kappa * bottom) / (base_diag + kappa)
    return bottom, surface_deep


def substitute(fresh_ref, ratio_ref, value_ref, bottom):
    layers = fresh_ref.shape[0]
    fresh_ref[layers - 1] = bottom

    def body(step, below):
        i = layers - 2 - step
        below = value_ref[i] + ratio_ref[i] * below
        fresh_ref[i] = below
        return below

    lax.fori_loop(0, layers - 1, body, bottom, unroll=7)


def seep(fresh_ref, rho_ref, fluid_ref, tally, kept_ref):
    layers = fresh_ref.shape[0]

    def body(i, flux):
        live = i < tally
        source = fluid_ref[i] + melt_rate * jnp.maximum(fresh_ref[i], 0.0)
        avail = jnp.where(live, source, 0.0) + flux
        kept = jnp.where(live, jnp.minimum(avail, holding_rate * (1.0 - rho_ref[i])), 0.0)
        kept_ref[i] = kept
        return avail - kept

    return lax.fori_loop(0, layers, body, jnp.zeros(tally.shape, jnp.float32), unroll=5)


def deep_return(returned, owner_col, position, devices):
    slots = position.shape[0]
    pick = jnp.where(lanes_of((slots, devices)) == owner_col, 1.0, 0.0)
    found = dot(pick, returned, NN, HIGH)
    lane = lanes_of((slots, LANES))
    return as_row(jnp.sum(jnp.where(lane == position, found, 0.0), axis=1, keepdims=True))


def deep_substitute(first, elink_ref, dprime_ref, rprime_ref, out_ref):
    layers = out_ref.shape[0]
    inverse = 1.0 / dprime_ref[...]
    rprime_ref[...] = rprime_ref[...] * inverse
    dprime_ref[1:layers, :] = elink_ref[0 : layers - 1, :] * inverse[1:]
    out_ref[0:1, :] = first

    def body(j, above):
        row = pl.ds(j, 1)
        above = rprime_ref[row, :] + dprime_ref[row, :] * above
        out_ref[row, :] = above
        return above

    lax.fori_loop(1, layers, body, first, unroll=7)


def start_kernel(
    devices, columns, temp_ref, rho_ref, pile_row_ref, pile_col_ref, own_ref, next_ref,
    elink_ref, dprime_ref, rprime_ref, message_ref, own_rank_ref, next_rank_ref,
    holder_ref, hit_ref, count_ref, a_ref, b_ref, p0_ref, p1_ref,
):
    diag, rhs = deep_eliminate(temp_ref, rho_ref, elink_ref, dprime_ref, rprime_ref)
    message_ref[:, 0:LANES] = deep_message(
        diag, rhs, pile_row_ref[...], pile_col_ref[...], columns, devices
    )
    rows = own_ref.shape[0]
    reaches = rows * LANES
    peer = reaches // devices
    holder_ref[...] = quotient(next_ref[...], reaches)
    ranks(holder_ref, next_rank_ref, hit_ref, count_ref, devices, rows)
    holder_ref[...] = quotient(own_ref[...], reaches)
    ranks(holder_ref, own_rank_ref, hit_ref, count_ref, devices, rows)
    position = remainder(own_ref[...], reaches)
    p0_ref[...] = quotient(position, LANES).astype(jnp.float32)
    p1_ref[...] = remainder(position, LANES).astype(jnp.float32)
    fill_places(b_ref, own_rank_ref, peer, rows)
    fill_values(a_ref, holder_ref, (p0_ref, p1_ref), devices, rows)
    high, low = placed_sum(a_ref, b_ref, devices, peer, reaches, 2)
    message_ref[:, LANES : LANES + peer] = high * LANES + low


def middle_kernel(
    devices, extents, origin_ref, snow_ref, east_ref, north_ref, temp_ref, rho_ref, size_ref,
    fluid_ref, tally_ref, air_ref, factor_ref, code_ref, own_ref, next_ref, own_rank_ref,
    next_rank_ref, got_ref, drift_ref, fresh_ref, kept_ref, answer_ref, ratio_ref, value_ref,
    a_ref, b_ref, high_ref, low_ref, p0_ref, p1_ref, p2_ref,
):
    tile_x, tile_y = tally_ref.shape
    snow = drift(
        snow_ref[...], east_ref[...], north_ref[...], tile_x, tile_y,
        origin_ref[0], origin_ref[1], extents[0], extents[1], STEPS,
    )
    drift_ref[...] = snow
    exchange = factor_ref[...] / (1.0 + snow)
    tally = tally_ref[...]
    carry = eliminate(
        temp_ref, rho_ref, size_ref, tally, exchange, air_ref[...], ratio_ref, value_ref
    )
    high, low, base_diag, base_rhs, flag = deep_places(got_ref[...], tile_x, tile_y)
    bottom, surface_deep = bottom_row(temp_ref, tally, carry, base_diag, base_rhs, flag)
    answer_ref[:, 0:LANES] = deep_answers(high, low, surface_deep, devices)
    substitute(fresh_ref, ratio_ref, value_ref, bottom)
    runoff = seep(fresh_ref, rho_ref, fluid_ref, tally, kept_ref)
    rows = own_ref.shape[0]
    reaches = rows * LANES
    peer = reaches // devices
    parts = (p0_ref, p1_ref, p2_ref)
    split_three(runoff, parts)
    high_ref[...] = quotient(code_ref[...], LANES)
    low_ref[...] = remainder(code_ref[...], LANES)
    fill_places(b_ref, low_ref, LANES, tile_x)
    fill_values(a_ref, high_ref, parts, 2 * rows, tile_x)
    binned = sum(placed_sum(a_ref, b_ref, 2 * rows, LANES, tile_x * LANES, 3))
    split_three(binned, parts)
    for half, (slot_ref, rank_ref) in enumerate(((own_ref, own_rank_ref), (next_ref, next_rank_ref))):
        high_ref[0:rows, :] = quotient(slot_ref[...], reaches)
        fill_places(b_ref, rank_ref, peer, rows)
        halves = [p.at[pl.ds(half * rows, rows)] for p in parts]
        fill_values(a_ref, high_ref, halves, devices, rows)
        lane = LANES + half * peer
        answer_ref[:, lane : lane + peer] = sum(placed_sum(a_ref, b_ref, devices, peer, reaches, 3))


def end_kernel(
    devices, columns, returned_ref, pile_row_ref, pile_col_ref, elink_ref, dprime_in, rprime_in,
    value_ref, place_ref, deep_ref, arrival_ref, dprime_ref, rprime_ref, a_ref, b_ref, high_ref,
    low_ref, p0_ref, p1_ref, p2_ref,
):
    owner_row, owner_col, position = deep_positions(pile_row_ref[...], pile_col_ref[...], columns)
    first = deep_return(returned_ref[...], owner_col, position, devices)
    dprime_ref[...] = dprime_in[...]
    rprime_ref[...] = rprime_in[...]
    deep_substitute(first, elink_ref, dprime_ref, rprime_ref, deep_ref)
    rows = value_ref.shape[0]
    parts = (p0_ref, p1_ref, p2_ref)
    split_three(value_ref[...], parts)
    place = place_ref[...]
    high_ref[...] = quotient(place, LANES)
    low_ref[...] = remainder(place, LANES)
    fill_places(b_ref, low_ref, LANES, rows)
    fill_values(a_ref, high_ref, parts, rows, rows)
    arrival_ref[...] = sum(placed_sum(a_ref, b_ref, rows, LANES, rows * LANES, 3))


def call(kernel, outs, scratch, smem_first=False):
    def run(*args):
        specs = [pl.BlockSpec(memory_space=pltpu.VMEM)] * len(args)
        if smem_first:
            specs[0] = pl.BlockSpec(memory_space=pltpu.SMEM)
        return pl.pallas_call(
            kernel,
            out_shape=[jax.ShapeDtypeStruct(s, d) for s, d in outs],
            in_specs=specs,
            out_specs=[pl.BlockSpec(memory_space=pltpu.VMEM)] * len(outs),
            scratch_shapes=[pltpu.VMEM(s, d) for s, d in scratch],
            compiler_params=pltpu.CompilerParams(vmem_limit_bytes=48 * 2**20),
        )(*args)

    return run


def halo_of(cells, axis, dim, width):
    count = lax.axis_size(axis)
    head = lax.slice_in_dim(cells, 0, width, axis=dim)
    tail = lax.slice_in_dim(cells, cells.shape[dim] - width, cells.shape[dim], axis=dim)
    before = lax.ppermute(tail, axis, [(i, i + 1) for i in range(count - 1)])
    after = lax.ppermute(head, axis, [(i + 1, i) for i in range(count - 1)])
    gap = list(cells.shape)
    gap[dim] = (-(cells.shape[dim] + 2 * width)) % (LANES if dim == 2 else 8)
    return jnp.concatenate([cells, after, jnp.zeros(gap, cells.dtype), before], axis=dim)


def local(
    stratum_warmth_celsius,
    stratum_mass_per_volume,
    stratum_melt_fluid,
    stratum_crystal_size,
    pile_stratum_tally,
    pile_atmospheric_warmth,
    topmost_thermal_factor,
    movable_topmost_powder,
    first_axis_gust_fraction,
    second_axis_gust_fraction,
    extra_stratum_warmth,
    extra_stratum_mass_per_volume,
    parent_pile,
    pile_stream_segment,
    segment_result_index,
):
    f32, i32, bf16 = jnp.float32, jnp.int32, jnp.bfloat16
    layers, tile_x, tile_y = stratum_warmth_celsius.shape
    deep_layers, slots = extra_stratum_warmth.shape
    tiles_x = lax.axis_size("gx")
    tiles_y = lax.axis_size("gy")
    devices = tiles_x * tiles_y
    columns = tile_x * tile_y
    reaches = segment_result_index.shape[0] // devices
    rows = reaches // LANES
    peer = reaches // devices
    extents = (tile_x * tiles_x, tile_y * tiles_y)
    gx, gy = lax.axis_index("gx"), lax.axis_index("gy")
    tile = gx * tiles_y + gy
    after = jnp.minimum(gx + 1, tiles_x - 1) * tiles_y + gy
    index = segment_result_index.reshape(devices * rows, LANES)
    own = lax.dynamic_slice_in_dim(index, tile * rows, rows, axis=0)
    following = lax.dynamic_slice_in_dim(index, after * rows, rows, axis=0)
    pile_row = parent_pile.reshape(1, slots)
    pile_col = parent_pile.reshape(slots, 1)

    fields = jnp.stack([movable_topmost_powder, first_axis_gust_fraction, second_axis_gust_fraction])
    fields = halo_of(fields, "gx", 1, STEPS)
    fields = halo_of(fields, "gy", 2, STEPS)

    wide = max(3 * 2 * rows, 3 * devices)
    elink, dprime, rprime, message, own_rank, next_rank = call(
        functools.partial(start_kernel, devices, columns),
        [((deep_layers, slots), f32)] * 3
        + [((devices, LANES + peer), f32), ((rows, LANES), i32), ((rows, LANES), i32)],
        [
            ((rows, LANES), i32),
            ((rows * devices, LANES), bf16),
            ((rows * devices, 2 * LANES), f32),
            ((2 * devices, reaches), bf16),
            ((peer, reaches), bf16),
            ((rows, LANES), f32),
            ((rows, LANES), f32),
        ],
    )(extra_stratum_warmth, extra_stratum_mass_per_volume, pile_row, pile_col, own, following)
    got = lax.all_to_all(message, ("gx", "gy"), split_axis=0, concat_axis=0, tiled=True)
    origin = jnp.stack([gx * tile_x, gy * tile_y]).astype(i32)
    drift_final, fresh, kept, answer = call(
        functools.partial(middle_kernel, devices, extents),
        [
            ((tile_x, tile_y), f32),
            ((layers, tile_x, tile_y), f32),
            ((layers, tile_x, tile_y), f32),
            ((devices, LANES + 2 * peer), f32),
        ],
        [
            ((layers, tile_x, tile_y), f32),
            ((layers, tile_x, tile_y), f32),
            ((wide, columns), bf16),
            ((LANES, columns), bf16),
            ((tile_x, LANES), i32),
            ((tile_x, LANES), i32),
        ]
        + [((tile_x, LANES), f32)] * 3,
        smem_first=True,
    )(
        origin, fields[0], fields[1], fields[2], stratum_warmth_celsius, stratum_mass_per_volume,
        stratum_crystal_size, stratum_melt_fluid, pile_stratum_tally, pile_atmospheric_warmth,
        topmost_thermal_factor, pile_stream_segment, own, following, own_rank, next_rank,
        got[:, 0:LANES],
    )
    back = lax.all_to_all(answer, ("gx", "gy"), split_axis=0, concat_axis=0, tiled=True)
    straight = back[:, LANES : LANES + peer]
    shifted = back[: devices - tiles_y, LANES + peer :]
    total = straight + jnp.pad(shifted, ((tiles_y, 0), (0, 0)))
    place = got[:, LANES:].astype(i32)
    deep_fresh, arrival = call(
        functools.partial(end_kernel, devices, columns),
        [((deep_layers, slots), f32), ((rows, LANES), f32)],
        [
            ((deep_layers, slots), f32),
            ((deep_layers, slots), f32),
            ((3 * rows, reaches), bf16),
            ((LANES, reaches), bf16),
            ((rows, LANES), i32),
            ((rows, LANES), i32),
        ]
        + [((rows, LANES), f32)] * 3,
    )(
        back[:, 0:LANES], pile_row, pile_col, elink, dprime, rprime,
        total.reshape(rows, LANES), place.reshape(rows, LANES),
    )
    return drift_final, fresh, kept, deep_fresh, arrival.reshape(reaches)


def solution(mesh):
    cells = P("gx", "gy")
    strata = P(None, "gx", "gy")
    deep = P(None, ("gx", "gy"))
    return jax.shard_map(
        local,
        mesh=mesh,
        in_specs=(strata,) * 4 + (cells,) * 6 + (deep, deep, P(("gx", "gy")), cells, P()),
        out_specs=(cells, strata, strata, deep, P(("gx", "gy"))),
        check_vma=False,
    )
```

```python
import functools

import jax
import jax.numpy as jnp
from jax import lax
from jax.experimental import pallas as pl
from jax.experimental.pallas import tpu as pltpu
from jax.sharding import PartitionSpec as P

STEPS = 4
PAIR = 8
LANES = 128

diffusion_number = 0.1
melt_rate = 0.02
holding_rate = 0.03

HIGH = lax.Precision.HIGHEST
NT = (((1,), (1,)), ((), ()))
TN = (((0,), (0,)), ((), ()))
NN = (((1,), (0,)), ((), ()))


def quotient(x, size):
    if size & (size - 1) == 0:
        return lax.shift_right_logical(x, jnp.full_like(x, size.bit_length() - 1))
    return lax.div(x, jnp.full_like(x, size))


def remainder(x, size):
    if size & (size - 1) == 0:
        return x & (size - 1)
    return lax.rem(x, jnp.full_like(x, size))


def rows_of(shape):
    return lax.broadcasted_iota(jnp.int32, shape, 0)


def lanes_of(shape):
    return lax.broadcasted_iota(jnp.int32, shape, 1)


def dot(a, b, dims, precision=None):
    return lax.dot_general(a, b, dims, precision=precision, preferred_element_type=jnp.float32)


def lane_chunk(i):
    return pl.ds(pl.multiple_of(i * LANES, LANES), LANES)


def fill_places(out_ref, index_ref, places, rows, unroll=4):
    def body(i, carry):
        hit = rows_of((places, LANES)) == index_ref[pl.ds(i, 1), :]
        out_ref[0:places, lane_chunk(i)] = jnp.where(hit, 1.0, 0.0).astype(jnp.bfloat16)
        return carry

    lax.fori_loop(0, rows, body, 0, unroll=unroll)


def fill_values(out_ref, index_ref, part_refs, places, rows, unroll=4):
    def body(i, carry):
        hit = rows_of((places, LANES)) == index_ref[pl.ds(i, 1), :]
        for p, part_ref in enumerate(part_refs):
            out_ref[p * places : (p + 1) * places, lane_chunk(i)] = jnp.where(
                hit, part_ref[pl.ds(i, 1), :], 0.0
            ).astype(jnp.bfloat16)
        return carry

    lax.fori_loop(0, rows, body, 0, unroll=unroll)


def split_three(value, part_refs):
    first = value.astype(jnp.bfloat16).astype(jnp.float32)
    second = (value - first).astype(jnp.bfloat16).astype(jnp.float32)
    rows = value.shape[0]
    part_refs[0][0:rows, :] = first
    part_refs[1][0:rows, :] = second
    part_refs[2][0:rows, :] = value - first - second


def placed_sum(a_ref, b_ref, places, lanes, width, parts):
    both = dot(a_ref[0 : parts * places, 0:width], b_ref[0:lanes, 0:width], NT)
    return [both[p * places : (p + 1) * places] for p in range(parts)]


def deep_eliminate(temp_ref, rho_ref, elink_ref, dprime_ref, rprime_ref):
    layers = temp_ref.shape[0]
    kdeep = 1.0 + 24.0 * rho_ref[...] * rho_ref[...]
    elink_ref[0 : layers - 1, :] = 0.5 * (kdeep[:-1] + kdeep[1:])
    elink_ref[layers - 1 : layers, :] = jnp.zeros_like(kdeep[:1])
    elink = elink_ref[...]
    dprime_ref[...] = 1.0 + elink
    dprime_ref[1:layers, :] = dprime_ref[1:layers, :] + elink[:-1]
    last = pl.ds(layers - 1, 1)
    diag = dprime_ref[last, :] + kdeep[layers - 1 :]
    rhs = temp_ref[last, :]
    dprime_ref[last, :] = diag
    rprime_ref[last, :] = rhs

    def body(step, carry):
        diag, rhs = carry
        row = pl.ds(layers - 2 - step, 1)
        link = elink_ref[row, :]
        ratio = link / diag
        diag = dprime_ref[row, :] - link * ratio
        rhs = temp_ref[row, :] + ratio * rhs
        dprime_ref[row, :] = diag
        rprime_ref[row, :] = rhs
        return diag, rhs

    return lax.fori_loop(0, layers - 1, body, (diag, rhs), unroll=7)


def deep_positions(pile_row, columns):
    slots = pile_row.shape[1]
    pile_col = as_column(pile_row.astype(jnp.float32)).astype(jnp.int32)
    owner_row = quotient(pile_row, columns)
    owner_col = quotient(pile_col, columns)
    square = (slots, slots)
    earlier = (owner_row == owner_col) & (lanes_of(square) < rows_of(square))
    position = jnp.sum(jnp.where(earlier, 1.0, 0.0), axis=1, keepdims=True).astype(jnp.int32)
    return owner_row, owner_col, remainder(pile_col, columns), position


def as_column(row):
    size = row.shape[1]
    eye = rows_of((size, size)) == lanes_of((size, size))
    return jnp.sum(jnp.where(eye, row, 0.0), axis=1, keepdims=True)


def as_row(column):
    size = column.shape[0]
    eye = rows_of((size, size)) == lanes_of((size, size))
    return jnp.sum(jnp.where(eye, column, 0.0), axis=0, keepdims=True)


def deep_message(diag, rhs, owner_row, cell, position, devices):
    slots = owner_row.shape[1]
    lane = lanes_of((slots, LANES))
    cell = (cell + 1).astype(jnp.float32)
    table = jnp.where(lane == position, as_column(diag), 0.0)
    table = jnp.where(lane == position + PAIR, as_column(rhs), table)
    table = jnp.where(lane == position + 2 * PAIR, cell, table)
    pick = jnp.where(rows_of((devices, slots)) == owner_row, 1.0, 0.0)
    return dot(pick, table, NN, HIGH)


def ranks(holder_ref, rank_ref, hit_ref, count_ref, devices, rows):
    def fill(i, carry):
        hit = rows_of((devices, LANES)) == holder_ref[pl.ds(i, 1), :]
        place = pl.ds(pl.multiple_of(i * devices, devices), devices)
        hit_ref[place, :] = jnp.where(hit, 1.0, 0.0).astype(jnp.bfloat16)
        return carry

    lax.fori_loop(0, rows, fill, 0, unroll=4)
    shape = (LANES, 2 * LANES)
    before = (rows_of(shape) < lanes_of(shape)) | (lanes_of(shape) >= LANES)
    count_ref[...] = dot(hit_ref[...], jnp.where(before, 1.0, 0.0).astype(jnp.bfloat16), NN)

    def number(i, base):
        hit = rows_of((devices, LANES)) == holder_ref[pl.ds(i, 1), :]
        place = pl.ds(pl.multiple_of(i * devices, devices), devices)
        count = count_ref[place, 0:LANES] + base
        rank_ref[pl.ds(i, 1), :] = jnp.sum(
            jnp.where(hit, count, 0.0), axis=0, keepdims=True
        ).astype(jnp.int32)
        return base + count_ref[place, LANES : 2 * LANES]

    lax.fori_loop(0, rows, number, jnp.zeros((devices, LANES), jnp.float32), unroll=4)


def drift(snow, east, north, tile_x, tile_y, first_x, first_y, extent_x, extent_y, halo):
    shape = snow.shape
    x = rows_of(shape)
    y = lanes_of(shape)
    x = first_x + jnp.where(x >= tile_x + halo, x - shape[0], x)
    y = first_y + jnp.where(y >= tile_y + halo, y - shape[1], y)
    inside = (x >= 0) & (x < extent_x) & (y >= 0) & (y < extent_y)
    east_up, east_down = jnp.maximum(east, 0.0), jnp.minimum(east, 0.0)
    north_up, north_down = jnp.maximum(north, 0.0), jnp.minimum(north, 0.0)
    snow = jnp.where(inside, snow, 0.0)
    for step in range(STEPS):
        before_x = pltpu.roll(snow, 1, 0)
        after_x = pltpu.roll(snow, shape[0] - 1, 0)
        before_y = pltpu.roll(snow, 1, 1)
        after_y = pltpu.roll(snow, shape[1] - 1, 1)
        change = -east_up * (snow - before_x) - east_down * (after_x - snow)
        change = change - north_up * (snow - before_y) - north_down * (after_y - snow)
        snow = (
            snow
            + change
            + diffusion_number * (before_x + after_x + before_y + after_y - 4.0 * snow)
        )
        snow = jnp.where(inside, snow, 0.0)
    return snow[0:tile_x, 0:tile_y]


def deep_places(got, tile_x, tile_y):
    devices = got.shape[0]
    highs, lows, diags, rhss = [], [], [], []
    for k in range(PAIR):
        cell = got[:, 2 * PAIR + k : 2 * PAIR + k + 1].astype(jnp.int32) - 1
        full = cell >= 0
        cell = jnp.maximum(cell, 0)
        high = (lanes_of((devices, tile_x)) == quotient(cell, tile_y)) & full
        low = (lanes_of((devices, tile_y)) == remainder(cell, tile_y)) & full
        highs.append(jnp.where(high, 1.0, 0.0))
        low = jnp.where(low, 1.0, 0.0)
        lows.append(low)
        diags.append(low * got[:, k : k + 1])
        rhss.append(low * got[:, PAIR + k : PAIR + k + 1])
    high = jnp.concatenate(highs, axis=0)
    low = jnp.concatenate(lows, axis=0)
    table = jnp.concatenate(
        [jnp.concatenate(diags, axis=0), jnp.concatenate(rhss, axis=0), low], axis=1
    )
    dense = dot(high, table, TN, HIGH)
    return (
        high,
        low,
        dense[:, 0:tile_y],
        dense[:, tile_y : 2 * tile_y],
        dense[:, 2 * tile_y :],
    )


def deep_answers(high, low, dense, devices):
    found = dot(high, dense, NN, HIGH) * low
    lane = lanes_of((devices, LANES))
    answer = jnp.zeros((devices, LANES), jnp.float32)
    for k in range(PAIR):
        value = jnp.sum(found[k * devices : (k + 1) * devices], axis=1, keepdims=True)
        answer = jnp.where(lane == k, value, answer)
    return answer


def eliminate(temp_ref, rho_ref, size_ref, tally, exchange, air, ratio_ref, value_ref):
    layers = temp_ref.shape[0]

    def kappa_of(i):
        rho = rho_ref[i]
        return 1.0 + 24.0 * rho * rho * size_ref[i]

    def row(i, kappa, up, ratio, value, diag_more, rhs_more):
        kappa_next = kappa_of(i + 1)
        down = jnp.where(i + 1 < tally, 0.5 * (kappa + kappa_next), 0.0)
        diag = 1.0 + up + down + jnp.where(i == tally - 1, kappa, 0.0)
        rhs = temp_ref[i]
        if diag_more is not None:
            diag = diag + diag_more
            rhs = rhs + rhs_more
        inverse = 1.0 / (diag - up * ratio)
        value = (rhs + up * value) * inverse
        ratio = down * inverse
        ratio_ref[i] = ratio
        value_ref[i] = value
        return kappa_next, down, ratio, value

    zero = jnp.zeros_like(air)
    carry = row(0, kappa_of(0), zero, zero, zero, exchange, exchange * air)
    return lax.fori_loop(
        1, layers - 1, lambda i, c: row(i, *c, None, None), carry, unroll=2
    )


def bottom_row(temp_ref, tally, carry, base_diag, base_rhs, flag):
    layers = temp_ref.shape[0]
    kappa, up, ratio, value = carry
    scale = flag * kappa / (base_diag + kappa)
    diag = 1.0 + up + jnp.where(tally == layers, kappa, 0.0) - scale * kappa
    rhs = temp_ref[layers - 1] + scale * base_rhs
    bottom = (rhs + up * value) / (diag - up * ratio)
    surface_deep = (base_rhs + kappa * bottom) / (base_diag + kappa)
    return bottom, surface_deep


def substitute(fresh_ref, ratio_ref, value_ref, bottom):
    layers = fresh_ref.shape[0]
    fresh_ref[layers - 1] = bottom

    def body(step, below):
        i = layers - 2 - step
        below = value_ref[i] + ratio_ref[i] * below
        fresh_ref[i] = below
        return below

    lax.fori_loop(0, layers - 1, body, bottom, unroll=7)


def seep(fresh_ref, rho_ref, fluid_ref, tally, kept_ref):
    layers = fresh_ref.shape[0]

    def body(i, flux):
        live = i < tally
        source = fluid_ref[i] + melt_rate * jnp.maximum(fresh_ref[i], 0.0)
        avail = jnp.where(live, source, 0.0) + flux
        kept = jnp.where(live, jnp.minimum(avail, holding_rate * (1.0 - rho_ref[i])), 0.0)
        kept_ref[i] = kept
        return avail - kept

    return lax.fori_loop(0, layers, body, jnp.zeros(tally.shape, jnp.float32), unroll=5)


def deep_return(returned, owner_col, position, devices):
    slots = position.shape[0]
    pick = jnp.where(lanes_of((slots, devices)) == owner_col, 1.0, 0.0)
    found = dot(pick, returned, NN, HIGH)
    lane = lanes_of((slots, LANES))
    return as_row(jnp.sum(jnp.where(lane == position, found, 0.0), axis=1, keepdims=True))


def deep_substitute(first, elink_ref, dprime_ref, rprime_ref, out_ref):
    layers = out_ref.shape[0]
    inverse = 1.0 / dprime_ref[...]
    rprime_ref[...] = rprime_ref[...] * inverse
    dprime_ref[1:layers, :] = elink_ref[0 : layers - 1, :] * inverse[1:]
    out_ref[0:1, :] = first

    def body(j, above):
        row = pl.ds(j, 1)
        above = rprime_ref[row, :] + dprime_ref[row, :] * above
        out_ref[row, :] = above
        return above

    lax.fori_loop(1, layers, body, first, unroll=7)


def peer_id(peer, tiles_y):
    return {"gx": lax.div(peer, tiles_y), "gy": lax.rem(peer, tiles_y)}


def row_copy(send_ref, got_ref, sems, source, target, device, tiles_y):
    return pltpu.make_async_remote_copy(
        src_ref=send_ref.at[source],
        dst_ref=got_ref.at[target],
        send_sem=sems.at[0],
        recv_sem=sems.at[1],
        device_id=peer_id(device, tiles_y),
        device_id_type=pl.DeviceIdType.MESH,
    )


def send_rows(send_ref, got_ref, sems, me, devices, tiles_y):
    def body(step, carry):
        peer = lax.rem(me + step, devices)
        row_copy(send_ref, got_ref, sems, peer, me, peer, tiles_y).start()
        return carry

    lax.fori_loop(1, devices, body, 0)


def rows_all(send_ref, got_ref, sems, me, devices, tiles_y):
    every = pl.ds(0, devices - 1)
    return row_copy(send_ref, got_ref, sems, every, every, lax.rem(me + 1, devices), tiles_y)


def got_rows(send_ref, got_ref, sems, me, devices, tiles_y):
    rows_all(send_ref, got_ref, sems, me, devices, tiles_y).wait_recv()
    got_ref[pl.ds(me, 1)] = send_ref[pl.ds(me, 1)]


def pack_sides(fields, strip_ref):
    shape = fields[0].shape
    lane = lanes_of(shape)
    packed = jnp.zeros(shape, jnp.float32)
    for f, field in enumerate(fields):
        first = 4 * f
        last = 16 + 4 * f
        moved = pltpu.roll(field, first, 1) if first else field
        packed = jnp.where((lane >= first) & (lane < first + STEPS), moved, packed)
        moved = pltpu.roll(field, STEPS + last, 1)
        packed = jnp.where((lane >= last) & (lane < last + STEPS), moved, packed)
    strip_ref[...] = packed


def joined_fields(fields, before_x, after_x, sides_after, sides_before):
    lane = lanes_of(sides_after.shape)
    out = []
    for f, field in enumerate(fields):
        ends = jnp.where(rows_of(after_x[f].shape) < STEPS, after_x[f], before_x[f])
        core = jnp.concatenate([field, ends], axis=0)
        first = 4 * f
        last = 16 + 4 * f
        after_y = pltpu.roll(sides_after, LANES - first, 1) if first else sides_after
        before_y = pltpu.roll(sides_before, LANES - STEPS - last, 1)
        side = jnp.where(lane < STEPS, after_y, jnp.where(lane >= LANES - STEPS, before_y, 0.0))
        out.append(jnp.concatenate([core, side], axis=1))
    return out


def step_kernel(
    tiles_x, tiles_y,
    temp_hbm, rho_hbm, size_hbm, fluid_hbm, tally_ref, air_ref, factor_ref, snow_ref, east_ref,
    north_ref, deep_temp_ref, deep_rho_ref, pile_ref, code_ref, index_hbm,
    drift_ref, fresh_hbm, kept_hbm, deep_ref, arrival_ref,
    temp_ref, rho_ref, size_ref, fluid_ref, own_ref, next_ref, ratio_ref, value_ref,
    elink_ref, dprime_ref, rprime_ref, strip_x_ref, strip_y_ref, got_x_ref, got_y_ref, got_d_ref,
    deep_send, deep_got, place_send, place_got, answer_send, answer_got, run_send, run_got,
    hit_ref, count_ref, own_rank_ref, next_rank_ref, own_holder_ref, next_holder_ref,
    own_b_ref, next_b_ref, code_b_ref, end_b_ref, a_ref, high_ref, low_ref, end_high_ref,
    end_low_ref, p0_ref, p1_ref, p2_ref, in_sems, out_sems, halo_send, halo_got, deep_sems,
    place_sems, answer_sems, run_sems,
):
    devices = tiles_x * tiles_y
    tile_x, tile_y = tally_ref.shape
    columns = tile_x * tile_y
    rows = own_ref.shape[0]
    reaches = rows * LANES
    gx, gy = lax.axis_index("gx"), lax.axis_index("gy")
    me = gx * tiles_y + gy
    follow = jnp.minimum(gx + 1, tiles_x - 1) * tiles_y + gy

    barrier = pltpu.get_barrier_semaphore()

    def greet(step, carry):
        pl.semaphore_signal(
            barrier, inc=1, device_id=peer_id(lax.rem(me + step, devices), tiles_y),
            device_id_type=pl.DeviceIdType.MESH,
        )
        return carry

    lax.fori_loop(1, devices, greet, 0)
    loads = [
        pltpu.make_async_copy(source, target, in_sems.at[k])
        for k, (source, target) in enumerate(
            (
                (index_hbm.at[pl.ds(pl.multiple_of(me * rows, 8), rows)], own_ref),
                (index_hbm.at[pl.ds(pl.multiple_of(follow * rows, 8), rows)], next_ref),
                (temp_hbm, temp_ref),
                (rho_hbm, rho_ref),
                (size_hbm, size_ref),
                (fluid_hbm, fluid_ref),
            )
        )
    ]
    for load in loads:
        load.start()

    edge = 2 * STEPS
    fields = (snow_ref[...], east_ref[...], north_ref[...])
    for f, field in enumerate(fields):
        strip_x_ref[0, f] = field[0:edge]
        strip_x_ref[1, f] = field[tile_x - edge : tile_x]
    pack_sides(fields, strip_y_ref)
    diag, rhs = deep_eliminate(deep_temp_ref, deep_rho_ref, elink_ref, dprime_ref, rprime_ref)
    owner_row, owner_col, cell, position = deep_positions(pile_ref[...], columns)
    deep_send[:, 0, :] = deep_message(diag, rhs, owner_row, cell, position, devices)

    pl.semaphore_wait(barrier, devices - 1)
    up_x, down_x = lax.rem(gx + 1, tiles_x), lax.rem(gx + tiles_x - 1, tiles_x)
    up_y, down_y = lax.rem(gy + 1, tiles_y), lax.rem(gy + tiles_y - 1, tiles_y)
    head = strip_y_ref.at[pl.ds(0, edge)]
    tail = strip_y_ref.at[pl.ds(tile_x - edge, edge)]
    halos = [
        pltpu.make_async_remote_copy(
            src_ref=source, dst_ref=target, send_sem=halo_send.at[k], recv_sem=halo_got.at[k],
            device_id={"gx": x, "gy": y}, device_id_type=pl.DeviceIdType.MESH,
        )
        for k, (source, target, x, y) in enumerate(
            (
                (strip_x_ref.at[1], got_x_ref.at[0], up_x, gy),
                (strip_x_ref.at[0], got_x_ref.at[1], down_x, gy),
                (strip_y_ref, got_y_ref.at[0], gx, up_y),
                (strip_y_ref, got_y_ref.at[1], gx, down_y),
                (tail, got_d_ref.at[0], up_x, up_y),
                (tail, got_d_ref.at[1], up_x, down_y),
                (head, got_d_ref.at[2], down_x, up_y),
                (head, got_d_ref.at[3], down_x, down_y),
            )
        )
    ]
    for halo in halos:
        halo.start()
    send_rows(deep_send, deep_got, deep_sems, me, devices, tiles_y)

    loads[0].wait()
    loads[1].wait()
    own_holder_ref[...] = quotient(own_ref[...], reaches)
    next_holder_ref[...] = quotient(next_ref[...], reaches)
    ranks(own_holder_ref, own_rank_ref, hit_ref, count_ref, devices, rows)
    fill_places(own_b_ref, own_rank_ref, LANES, rows)
    spot = remainder(own_ref[...], reaches)
    p0_ref[0:rows, :] = quotient(spot, LANES).astype(jnp.float32)
    p1_ref[0:rows, :] = remainder(spot, LANES).astype(jnp.float32)
    fill_values(a_ref, own_holder_ref, (p0_ref, p1_ref), devices, rows)
    high, low = placed_sum(a_ref, own_b_ref, devices, LANES, reaches, 2)
    place_send[:, 0, :] = high * LANES + low
    send_rows(place_send, place_got, place_sems, me, devices, tiles_y)

    for halo in halos:
        halo.wait_recv()
    near = rows_of((edge, LANES)) < STEPS
    corner_after = jnp.where(near, got_d_ref[3], got_d_ref[1])
    corner_before = jnp.where(near, got_d_ref[2], got_d_ref[0])
    snow, east, north = joined_fields(
        fields,
        [got_x_ref[0, f] for f in range(3)],
        [got_x_ref[1, f] for f in range(3)],
        jnp.concatenate([got_y_ref[1], corner_after], axis=0),
        jnp.concatenate([got_y_ref[0], corner_before], axis=0),
    )
    snow = drift(
        snow, east, north, tile_x, tile_y, gx * tile_x, gy * tile_y,
        tile_x * tiles_x, tile_y * tiles_y, STEPS,
    )
    drift_ref[...] = snow
    exchange = factor_ref[...] / (1.0 + snow)
    tally = tally_ref[...]
    for load in loads[2:]:
        load.wait()
    carry = eliminate(
        temp_ref, rho_ref, size_ref, tally, exchange, air_ref[...], ratio_ref, value_ref
    )

    got_rows(deep_send, deep_got, deep_sems, me, devices, tiles_y)
    high, low, base_diag, base_rhs, flag = deep_places(deep_got[:, 0, :], tile_x, tile_y)
    bottom, surface_deep = bottom_row(temp_ref, tally, carry, base_diag, base_rhs, flag)
    answer_send[:, 0, :] = deep_answers(high, low, surface_deep, devices)
    send_rows(answer_send, answer_got, answer_sems, me, devices, tiles_y)

    substitute(value_ref, ratio_ref, value_ref, bottom)
    fresh_out = pltpu.make_async_copy(value_ref, fresh_hbm, out_sems.at[0])
    fresh_out.start()
    runoff = seep(value_ref, rho_ref, fluid_ref, tally, fluid_ref)
    kept_out = pltpu.make_async_copy(fluid_ref, kept_hbm, out_sems.at[1])
    kept_out.start()

    parts = (p0_ref, p1_ref, p2_ref)
    ranks(next_holder_ref, next_rank_ref, hit_ref, count_ref, devices, rows)
    fill_places(next_b_ref, next_rank_ref, LANES, rows)
    high_ref[...] = quotient(code_ref[...], LANES)
    low_ref[...] = remainder(code_ref[...], LANES)
    fill_places(code_b_ref, low_ref, LANES, tile_x)
    split_three(runoff, parts)
    fill_values(a_ref, high_ref, parts, 2 * rows, tile_x)
    binned = sum(placed_sum(a_ref, code_b_ref, 2 * rows, LANES, columns, 3))
    split_three(binned, parts)
    for half, (holder_ref, b_ref) in enumerate(
        ((own_holder_ref, own_b_ref), (next_holder_ref, next_b_ref))
    ):
        halves = [p.at[pl.ds(half * rows, rows)] for p in parts]
        fill_values(a_ref, holder_ref, halves, devices, rows)
        run_send[:, 0, half * LANES : (half + 1) * LANES] = sum(
            placed_sum(a_ref, b_ref, devices, LANES, reaches, 3)
        )
    send_rows(run_send, run_got, run_sems, me, devices, tiles_y)

    got_rows(answer_send, answer_got, answer_sems, me, devices, tiles_y)
    first = deep_return(answer_got[:, 0, :], owner_col, position, devices)
    deep_substitute(first, elink_ref, dprime_ref, rprime_ref, deep_ref)
    got_rows(place_send, place_got, place_sems, me, devices, tiles_y)
    place = place_got[:, 0, :].astype(jnp.int32)
    end_high_ref[...] = quotient(place, LANES)
    end_low_ref[...] = remainder(place, LANES)
    fill_places(end_b_ref, end_low_ref, LANES, devices)
    got_rows(run_send, run_got, run_sems, me, devices, tiles_y)
    behind = pltpu.roll(run_got[:, 0, LANES:], tiles_y, 0)
    behind = jnp.where(rows_of(behind.shape) >= tiles_y, behind, 0.0)
    ends = [p.at[pl.ds(0, devices)] for p in parts]
    split_three(run_got[:, 0, 0:LANES] + behind, ends)
    fill_values(a_ref, end_high_ref, ends, rows, devices)
    arrival_ref[...] = sum(placed_sum(a_ref, end_b_ref, rows, LANES, devices * LANES, 3))

    for halo in halos:
        halo.wait_send()
    for send_ref, got_ref, sems in (
        (deep_send, deep_got, deep_sems), (place_send, place_got, place_sems),
        (answer_send, answer_got, answer_sems), (run_send, run_got, run_sems),
    ):
        rows_all(send_ref, got_ref, sems, me, devices, tiles_y).wait_send()
    fresh_out.wait()
    kept_out.wait()


def local(*args):
    f32, i32, bf16 = jnp.float32, jnp.int32, jnp.bfloat16
    layers, tile_x, tile_y = args[0].shape
    deep_layers, slots = args[10].shape
    tiles_x = lax.axis_size("gx")
    tiles_y = lax.axis_size("gy")
    devices = tiles_x * tiles_y
    columns = tile_x * tile_y
    reaches = args[14].shape[0] // devices
    rows = reaches // LANES
    strata = (layers, tile_x, tile_y)
    deep = (deep_layers, slots)
    edge = 2 * STEPS
    wide = max(3 * 2 * rows, 3 * devices)
    width = max(columns, devices * LANES)
    tall = max(tile_x, 2 * rows, devices)
    grid = (rows, LANES)
    message = (devices, 1, LANES)
    scratch = (
        [(strata, f32)] * 4
        + [(grid, i32)] * 2
        + [(strata, f32)] * 2
        + [(deep, f32)] * 3
        + [((2, 3, edge, tile_y), f32), ((tile_x, tile_y), f32), ((2, 3, edge, tile_y), f32)]
        + [((2, tile_x, tile_y), f32), ((4, edge, tile_y), f32)]
        + [(message, f32)] * 6
        + [((devices, 1, 2 * LANES), f32)] * 2
        + [((rows * devices, LANES), bf16), ((rows * devices, 2 * LANES), f32)]
        + [(grid, i32)] * 4
        + [((LANES, reaches), bf16)] * 2
        + [((LANES, columns), bf16), ((LANES, devices * LANES), bf16), ((wide, width), bf16)]
        + [((tile_x, tile_y), i32)] * 2
        + [((devices, LANES), i32)] * 2
        + [((tall, LANES), f32)] * 3
    )
    dma = pltpu.SemaphoreType.DMA
    vmem = pl.BlockSpec(memory_space=pltpu.VMEM)
    anywhere = pl.BlockSpec(memory_space=pl.ANY)
    outs = ((tile_x, tile_y), strata, strata, deep, grid)
    drift_final, fresh, kept, deep_fresh, arrival = pl.pallas_call(
        functools.partial(step_kernel, tiles_x, tiles_y),
        out_shape=[jax.ShapeDtypeStruct(s, f32) for s in outs],
        in_specs=[anywhere] * 4 + [vmem] * 10 + [anywhere],
        out_specs=[vmem, anywhere, anywhere, vmem, vmem],
        scratch_shapes=[pltpu.VMEM(s, d) for s, d in scratch]
        + [dma((6,)), dma((2,)), dma((8,)), dma((8,)), dma((2,)), dma((2,)), dma((2,)), dma((2,))],
        compiler_params=pltpu.CompilerParams(
            collective_id=0, has_side_effects=True, vmem_limit_bytes=56 * 2**20
        ),
    )(
        args[0], args[1], args[3], args[2], args[4], args[5], args[6], args[7], args[8], args[9],
        args[10], args[11], args[12].reshape(1, slots), args[13],
        args[14].reshape(devices * rows, LANES),
    )
    return drift_final, fresh, kept, deep_fresh, arrival.reshape(reaches)


def solution(mesh):
    cells = P("gx", "gy")
    strata = P(None, "gx", "gy")
    deep = P(None, ("gx", "gy"))
    return jax.shard_map(
        local,
        mesh=mesh,
        in_specs=(strata,) * 4 + (cells,) * 6 + (deep, deep, P(("gx", "gy")), cells, P()),
        out_specs=(cells, strata, strata, deep, P(("gx", "gy"))),
        check_vma=False,
    )
```

```python
import functools

import jax
import jax.numpy as jnp
from jax import lax
from jax.experimental import pallas as pl
from jax.experimental.pallas import tpu as pltpu
from jax.sharding import PartitionSpec as P

STEPS = 4
PAIR = 8
LANES = 128

diffusion_number = 0.1
melt_rate = 0.02
holding_rate = 0.03

HIGH = lax.Precision.HIGHEST
NT = (((1,), (1,)), ((), ()))
TN = (((0,), (0,)), ((), ()))
NN = (((1,), (0,)), ((), ()))


def quotient(x, size):
    if size & (size - 1) == 0:
        return lax.shift_right_logical(x, jnp.full_like(x, size.bit_length() - 1))
    return lax.div(x, jnp.full_like(x, size))


def remainder(x, size):
    if size & (size - 1) == 0:
        return x & (size - 1)
    return lax.rem(x, jnp.full_like(x, size))


def rows_of(shape):
    return lax.broadcasted_iota(jnp.int32, shape, 0)


def lanes_of(shape):
    return lax.broadcasted_iota(jnp.int32, shape, 1)


def dot(a, b, dims, precision=None):
    return lax.dot_general(a, b, dims, precision=precision, preferred_element_type=jnp.float32)


def lane_chunk(i):
    return pl.ds(pl.multiple_of(i * LANES, LANES), LANES)


def fill_places(out_ref, index_ref, places, rows, unroll=4):
    def body(i, carry):
        hit = rows_of((places, LANES)) == index_ref[pl.ds(i, 1), :]
        out_ref[0:places, lane_chunk(i)] = jnp.where(hit, 1.0, 0.0).astype(jnp.bfloat16)
        return carry

    lax.fori_loop(0, rows, body, 0, unroll=unroll)


def fill_values(out_ref, index_ref, part_refs, places, rows, unroll=4):
    def body(i, carry):
        hit = rows_of((places, LANES)) == index_ref[pl.ds(i, 1), :]
        for p, part_ref in enumerate(part_refs):
            out_ref[p * places : (p + 1) * places, lane_chunk(i)] = jnp.where(
                hit, part_ref[pl.ds(i, 1), :], 0.0
            ).astype(jnp.bfloat16)
        return carry

    lax.fori_loop(0, rows, body, 0, unroll=unroll)


def split_three(value, part_refs):
    first = value.astype(jnp.bfloat16).astype(jnp.float32)
    second = (value - first).astype(jnp.bfloat16).astype(jnp.float32)
    rows = value.shape[0]
    part_refs[0][0:rows, :] = first
    part_refs[1][0:rows, :] = second
    part_refs[2][0:rows, :] = value - first - second


def placed_sum(a_ref, b_ref, places, lanes, width, parts):
    both = dot(a_ref[0 : parts * places, 0:width], b_ref[0:lanes, 0:width], NT)
    return [both[p * places : (p + 1) * places] for p in range(parts)]


def deep_eliminate(temp_ref, rho_ref, elink_ref, dprime_ref, rprime_ref):
    layers = temp_ref.shape[0]
    kdeep = 1.0 + 24.0 * rho_ref[...] * rho_ref[...]
    elink_ref[0 : layers - 1, :] = 0.5 * (kdeep[:-1] + kdeep[1:])
    elink_ref[layers - 1 : layers, :] = jnp.zeros_like(kdeep[:1])
    elink = elink_ref[...]
    dprime_ref[...] = 1.0 + elink
    dprime_ref[1:layers, :] = dprime_ref[1:layers, :] + elink[:-1]
    last = pl.ds(layers - 1, 1)
    diag = dprime_ref[last, :] + kdeep[layers - 1 :]
    rhs = temp_ref[last, :]
    dprime_ref[last, :] = diag
    rprime_ref[last, :] = rhs

    def body(step, carry):
        diag, rhs = carry
        row = pl.ds(layers - 2 - step, 1)
        link = elink_ref[row, :]
        ratio = link / diag
        diag = dprime_ref[row, :] - link * ratio
        rhs = temp_ref[row, :] + ratio * rhs
        dprime_ref[row, :] = diag
        rprime_ref[row, :] = rhs
        return diag, rhs

    return lax.fori_loop(0, layers - 1, body, (diag, rhs), unroll=7)


def deep_positions(pile_row, columns):
    slots = pile_row.shape[1]
    pile_col = as_column(pile_row.astype(jnp.float32)).astype(jnp.int32)
    owner_row = quotient(pile_row, columns)
    owner_col = quotient(pile_col, columns)
    square = (slots, slots)
    earlier = (owner_row == owner_col) & (lanes_of(square) < rows_of(square))
    position = jnp.sum(jnp.where(earlier, 1.0, 0.0), axis=1, keepdims=True).astype(jnp.int32)
    return owner_row, owner_col, remainder(pile_col, columns), position


def as_column(row):
    size = row.shape[1]
    eye = rows_of((size, size)) == lanes_of((size, size))
    return jnp.sum(jnp.where(eye, row, 0.0), axis=1, keepdims=True)


def as_row(column):
    size = column.shape[0]
    eye = rows_of((size, size)) == lanes_of((size, size))
    return jnp.sum(jnp.where(eye, column, 0.0), axis=0, keepdims=True)


def deep_message(diag, rhs, owner_row, cell, position, devices):
    slots = owner_row.shape[1]
    lane = lanes_of((slots, LANES))
    cell = (cell + 1).astype(jnp.float32)
    table = jnp.where(lane == position, as_column(diag), 0.0)
    table = jnp.where(lane == position + PAIR, as_column(rhs), table)
    table = jnp.where(lane == position + 2 * PAIR, cell, table)
    pick = jnp.where(rows_of((devices, slots)) == owner_row, 1.0, 0.0)
    return dot(pick, table, NN, HIGH)


def ranks(holder_ref, rank_ref, hit_ref, count_ref, devices, rows):
    def fill(i, carry):
        hit = rows_of((devices, LANES)) == holder_ref[pl.ds(i, 1), :]
        place = pl.ds(pl.multiple_of(i * devices, devices), devices)
        hit_ref[place, :] = jnp.where(hit, 1.0, 0.0).astype(jnp.bfloat16)
        return carry

    lax.fori_loop(0, rows, fill, 0, unroll=4)
    shape = (LANES, 2 * LANES)
    before = (rows_of(shape) < lanes_of(shape)) | (lanes_of(shape) >= LANES)
    count_ref[...] = dot(hit_ref[...], jnp.where(before, 1.0, 0.0).astype(jnp.bfloat16), NN)

    def number(i, base):
        hit = rows_of((devices, LANES)) == holder_ref[pl.ds(i, 1), :]
        place = pl.ds(pl.multiple_of(i * devices, devices), devices)
        count = count_ref[place, 0:LANES] + base
        rank_ref[pl.ds(i, 1), :] = jnp.sum(
            jnp.where(hit, count, 0.0), axis=0, keepdims=True
        ).astype(jnp.int32)
        return base + count_ref[place, LANES : 2 * LANES]

    lax.fori_loop(0, rows, number, jnp.zeros((devices, LANES), jnp.float32), unroll=4)


def drift(snow, east, north, tile_x, tile_y, first_x, first_y, extent_x, extent_y, halo):
    shape = snow.shape
    x = rows_of(shape)
    y = lanes_of(shape)
    x = first_x + jnp.where(x >= tile_x + halo, x - shape[0], x)
    y = first_y + jnp.where(y >= tile_y + halo, y - shape[1], y)
    inside = (x >= 0) & (x < extent_x) & (y >= 0) & (y < extent_y)
    east_up, east_down = jnp.maximum(east, 0.0), jnp.minimum(east, 0.0)
    north_up, north_down = jnp.maximum(north, 0.0), jnp.minimum(north, 0.0)
    snow = jnp.where(inside, snow, 0.0)
    for step in range(STEPS):
        before_x = pltpu.roll(snow, 1, 0)
        after_x = pltpu.roll(snow, shape[0] - 1, 0)
        before_y = pltpu.roll(snow, 1, 1)
        after_y = pltpu.roll(snow, shape[1] - 1, 1)
        change = -east_up * (snow - before_x) - east_down * (after_x - snow)
        change = change - north_up * (snow - before_y) - north_down * (after_y - snow)
        snow = (
            snow
            + change
            + diffusion_number * (before_x + after_x + before_y + after_y - 4.0 * snow)
        )
        snow = jnp.where(inside, snow, 0.0)
    return snow[0:tile_x, 0:tile_y]


def deep_places(got, tile_x, tile_y):
    devices = got.shape[0]
    highs, lows, diags, rhss = [], [], [], []
    for k in range(PAIR):
        cell = got[:, 2 * PAIR + k : 2 * PAIR + k + 1].astype(jnp.int32) - 1
        full = cell >= 0
        cell = jnp.maximum(cell, 0)
        high = (lanes_of((devices, tile_x)) == quotient(cell, tile_y)) & full
        low = (lanes_of((devices, tile_y)) == remainder(cell, tile_y)) & full
        highs.append(jnp.where(high, 1.0, 0.0))
        low = jnp.where(low, 1.0, 0.0)
        lows.append(low)
        diags.append(low * got[:, k : k + 1])
        rhss.append(low * got[:, PAIR + k : PAIR + k + 1])
    high = jnp.concatenate(highs, axis=0)
    low = jnp.concatenate(lows, axis=0)
    table = jnp.concatenate(
        [jnp.concatenate(diags, axis=0), jnp.concatenate(rhss, axis=0), low], axis=1
    )
    dense = dot(high, table, TN, HIGH)
    return (
        high,
        low,
        dense[:, 0:tile_y],
        dense[:, tile_y : 2 * tile_y],
        dense[:, 2 * tile_y :],
    )


def deep_answers(high, low, dense, devices):
    found = dot(high, dense, NN, HIGH) * low
    lane = lanes_of((devices, LANES))
    answer = jnp.zeros((devices, LANES), jnp.float32)
    for k in range(PAIR):
        value = jnp.sum(found[k * devices : (k + 1) * devices], axis=1, keepdims=True)
        answer = jnp.where(lane == k, value, answer)
    return answer


def eliminate(temp_ref, rho_ref, size_ref, tally, exchange, air, ratio_ref, value_ref):
    layers = temp_ref.shape[0]

    def kappa_of(i):
        rho = rho_ref[i]
        return 1.0 + 24.0 * rho * rho * size_ref[i]

    def row(i, kappa, up, ratio, value, diag_more, rhs_more):
        kappa_next = kappa_of(i + 1)
        down = jnp.where(i + 1 < tally, 0.5 * (kappa + kappa_next), 0.0)
        diag = 1.0 + up + down + jnp.where(i == tally - 1, kappa, 0.0)
        rhs = temp_ref[i]
        if diag_more is not None:
            diag = diag + diag_more
            rhs = rhs + rhs_more
        inverse = 1.0 / (diag - up * ratio)
        value = (rhs + up * value) * inverse
        ratio = down * inverse
        ratio_ref[i] = ratio
        value_ref[i] = value
        return kappa_next, down, ratio, value

    zero = jnp.zeros_like(air)
    carry = row(0, kappa_of(0), zero, zero, zero, exchange, exchange * air)
    return lax.fori_loop(
        1, layers - 1, lambda i, c: row(i, *c, None, None), carry, unroll=2
    )


def bottom_row(temp_ref, tally, carry, base_diag, base_rhs, flag):
    layers = temp_ref.shape[0]
    kappa, up, ratio, value = carry
    scale = flag * kappa / (base_diag + kappa)
    diag = 1.0 + up + jnp.where(tally == layers, kappa, 0.0) - scale * kappa
    rhs = temp_ref[layers - 1] + scale * base_rhs
    bottom = (rhs + up * value) / (diag - up * ratio)
    surface_deep = (base_rhs + kappa * bottom) / (base_diag + kappa)
    return bottom, surface_deep


def substitute(fresh_ref, ratio_ref, value_ref, bottom):
    layers = fresh_ref.shape[0]
    fresh_ref[layers - 1] = bottom

    def body(step, below):
        i = layers - 2 - step
        below = value_ref[i] + ratio_ref[i] * below
        fresh_ref[i] = below
        return below

    lax.fori_loop(0, layers - 1, body, bottom, unroll=7)


def seep(fresh_ref, rho_ref, fluid_ref, tally, kept_ref):
    layers = fresh_ref.shape[0]

    def body(i, flux):
        live = i < tally
        source = fluid_ref[i] + melt_rate * jnp.maximum(fresh_ref[i], 0.0)
        avail = jnp.where(live, source, 0.0) + flux
        kept = jnp.where(live, jnp.minimum(avail, holding_rate * (1.0 - rho_ref[i])), 0.0)
        kept_ref[i] = kept
        return avail - kept

    return lax.fori_loop(0, layers, body, jnp.zeros(tally.shape, jnp.float32), unroll=5)


def deep_return(returned, owner_col, position, devices):
    slots = position.shape[0]
    pick = jnp.where(lanes_of((slots, devices)) == owner_col, 1.0, 0.0)
    found = dot(pick, returned, NN, HIGH)
    lane = lanes_of((slots, LANES))
    return as_row(jnp.sum(jnp.where(lane == position, found, 0.0), axis=1, keepdims=True))


def deep_substitute(first, elink_ref, dprime_ref, rprime_ref, out_ref):
    layers = out_ref.shape[0]
    inverse = 1.0 / dprime_ref[...]
    rprime_ref[...] = rprime_ref[...] * inverse
    dprime_ref[1:layers, :] = elink_ref[0 : layers - 1, :] * inverse[1:]
    out_ref[0:1, :] = first

    def body(j, above):
        row = pl.ds(j, 1)
        above = rprime_ref[row, :] + dprime_ref[row, :] * above
        out_ref[row, :] = above
        return above

    lax.fori_loop(1, layers, body, first, unroll=7)


def peer_id(peer, tiles_y):
    return {"gx": lax.div(peer, tiles_y), "gy": lax.rem(peer, tiles_y)}


def row_copy(send_ref, got_ref, sems, source, target, device, tiles_y):
    return pltpu.make_async_remote_copy(
        src_ref=send_ref.at[source],
        dst_ref=got_ref.at[target],
        send_sem=sems.at[0],
        recv_sem=sems.at[1],
        device_id=peer_id(device, tiles_y),
        device_id_type=pl.DeviceIdType.MESH,
    )


def send_rows(send_ref, got_ref, sems, me, devices, tiles_y):
    def body(step, carry):
        peer = lax.rem(me + step, devices)
        row_copy(send_ref, got_ref, sems, peer, me, peer, tiles_y).start()
        return carry

    lax.fori_loop(1, devices, body, 0, unroll=4)


def rows_all(send_ref, got_ref, sems, me, devices, tiles_y):
    every = pl.ds(0, devices - 1)
    return row_copy(send_ref, got_ref, sems, every, every, lax.rem(me + 1, devices), tiles_y)


def got_rows(send_ref, got_ref, sems, me, devices, tiles_y):
    rows_all(send_ref, got_ref, sems, me, devices, tiles_y).wait_recv()
    got_ref[pl.ds(me, 1)] = send_ref[pl.ds(me, 1)]


def pack_sides(fields, strip_ref):
    shape = fields[0].shape
    lane = lanes_of(shape)
    packed = jnp.zeros(shape, jnp.float32)
    for f, field in enumerate(fields):
        first = 4 * f
        last = 16 + 4 * f
        moved = pltpu.roll(field, first, 1) if first else field
        packed = jnp.where((lane >= first) & (lane < first + STEPS), moved, packed)
        moved = pltpu.roll(field, STEPS + last, 1)
        packed = jnp.where((lane >= last) & (lane < last + STEPS), moved, packed)
    strip_ref[...] = packed


def joined_fields(fields, before_x, after_x, sides_after, sides_before):
    lane = lanes_of(sides_after.shape)
    out = []
    for f, field in enumerate(fields):
        ends = jnp.where(rows_of(after_x[f].shape) < STEPS, after_x[f], before_x[f])
        core = jnp.concatenate([field, ends], axis=0)
        first = 4 * f
        last = 16 + 4 * f
        after_y = pltpu.roll(sides_after, LANES - first, 1) if first else sides_after
        before_y = pltpu.roll(sides_before, LANES - STEPS - last, 1)
        side = jnp.where(lane < STEPS, after_y, jnp.where(lane >= LANES - STEPS, before_y, 0.0))
        out.append(jnp.concatenate([core, side], axis=1))
    return out


def step_kernel(
    tiles_x, tiles_y,
    temp_hbm, rho_hbm, size_hbm, fluid_hbm, tally_ref, air_ref, factor_ref, snow_ref, east_ref,
    north_ref, deep_temp_ref, deep_rho_ref, pile_ref, code_ref, index_hbm,
    drift_ref, fresh_hbm, kept_hbm, deep_ref, total_ref, place_ref,
    temp_ref, rho_ref, size_ref, fluid_ref, own_ref, next_ref, ratio_ref, value_ref,
    elink_ref, dprime_ref, rprime_ref, strip_x_ref, strip_y_ref, got_x_ref, got_y_ref, got_d_ref,
    deep_send, deep_got, answer_send, answer_got, run_send, run_got,
    hit_ref, count_ref, own_rank_ref, next_rank_ref, own_holder_ref, next_holder_ref,
    own_b_ref, next_b_ref, code_b_ref, a_ref, high_ref, low_ref, p0_ref, p1_ref, p2_ref, in_sems, out_sems, halo_send, halo_got, deep_sems,
    answer_sems, run_sems,
):
    devices = tiles_x * tiles_y
    tile_x, tile_y = tally_ref.shape
    columns = tile_x * tile_y
    rows = own_ref.shape[0]
    reaches = rows * LANES
    gx, gy = lax.axis_index("gx"), lax.axis_index("gy")
    me = gx * tiles_y + gy
    follow = jnp.minimum(gx + 1, tiles_x - 1) * tiles_y + gy

    barrier = pltpu.get_barrier_semaphore()

    def greet(step, carry):
        pl.semaphore_signal(
            barrier, inc=1, device_id=peer_id(lax.rem(me + step, devices), tiles_y),
            device_id_type=pl.DeviceIdType.MESH,
        )
        return carry

    lax.fori_loop(1, devices, greet, 0)
    loads = [
        pltpu.make_async_copy(source, target, in_sems.at[k])
        for k, (source, target) in enumerate(
            (
                (index_hbm.at[pl.ds(pl.multiple_of(me * rows, 8), rows)], own_ref),
                (index_hbm.at[pl.ds(pl.multiple_of(follow * rows, 8), rows)], next_ref),
                (temp_hbm, temp_ref),
                (rho_hbm, rho_ref),
                (size_hbm, size_ref),
                (fluid_hbm, fluid_ref),
            )
        )
    ]
    for load in loads:
        load.start()

    edge = 2 * STEPS
    fields = (snow_ref[...], east_ref[...], north_ref[...])
    for f, field in enumerate(fields):
        strip_x_ref[0, f] = field[0:edge]
        strip_x_ref[1, f] = field[tile_x - edge : tile_x]
    pack_sides(fields, strip_y_ref)
    diag, rhs = deep_eliminate(deep_temp_ref, deep_rho_ref, elink_ref, dprime_ref, rprime_ref)
    owner_row, owner_col, cell, position = deep_positions(pile_ref[...], columns)
    deep_send[:, 0, 0:LANES] = deep_message(diag, rhs, owner_row, cell, position, devices)

    pl.semaphore_wait(barrier, devices - 1)
    up_x, down_x = lax.rem(gx + 1, tiles_x), lax.rem(gx + tiles_x - 1, tiles_x)
    up_y, down_y = lax.rem(gy + 1, tiles_y), lax.rem(gy + tiles_y - 1, tiles_y)
    head = strip_y_ref.at[pl.ds(0, edge)]
    tail = strip_y_ref.at[pl.ds(tile_x - edge, edge)]
    halos = [
        pltpu.make_async_remote_copy(
            src_ref=source, dst_ref=target, send_sem=halo_send.at[k], recv_sem=halo_got.at[k],
            device_id={"gx": x, "gy": y}, device_id_type=pl.DeviceIdType.MESH,
        )
        for k, (source, target, x, y) in enumerate(
            (
                (strip_x_ref.at[1], got_x_ref.at[0], up_x, gy),
                (strip_x_ref.at[0], got_x_ref.at[1], down_x, gy),
                (strip_y_ref, got_y_ref.at[0], gx, up_y),
                (strip_y_ref, got_y_ref.at[1], gx, down_y),
                (tail, got_d_ref.at[0], up_x, up_y),
                (tail, got_d_ref.at[1], up_x, down_y),
                (head, got_d_ref.at[2], down_x, up_y),
                (head, got_d_ref.at[3], down_x, down_y),
            )
        )
    ]
    for halo in halos:
        halo.start()

    loads[0].wait()
    loads[1].wait()
    own_holder_ref[...] = quotient(own_ref[...], reaches)
    next_holder_ref[...] = quotient(next_ref[...], reaches)
    ranks(own_holder_ref, own_rank_ref, hit_ref, count_ref, devices, rows)
    fill_places(own_b_ref, own_rank_ref, LANES, rows)
    spot = remainder(own_ref[...], reaches)
    p0_ref[0:rows, :] = quotient(spot, LANES).astype(jnp.float32)
    p1_ref[0:rows, :] = remainder(spot, LANES).astype(jnp.float32)
    fill_values(a_ref, own_holder_ref, (p0_ref, p1_ref), devices, rows)
    high, low = placed_sum(a_ref, own_b_ref, devices, LANES, reaches, 2)
    deep_send[:, 0, LANES:] = high * LANES + low
    send_rows(deep_send, deep_got, deep_sems, me, devices, tiles_y)
    ranks(next_holder_ref, next_rank_ref, hit_ref, count_ref, devices, rows)
    fill_places(next_b_ref, next_rank_ref, LANES, rows)
    high_ref[...] = quotient(code_ref[...], LANES)
    low_ref[...] = remainder(code_ref[...], LANES)
    fill_places(code_b_ref, low_ref, LANES, tile_x)

    for halo in halos:
        halo.wait_recv()
    near = rows_of((edge, LANES)) < STEPS
    corner_after = jnp.where(near, got_d_ref[3], got_d_ref[1])
    corner_before = jnp.where(near, got_d_ref[2], got_d_ref[0])
    snow, east, north = joined_fields(
        fields,
        [got_x_ref[0, f] for f in range(3)],
        [got_x_ref[1, f] for f in range(3)],
        jnp.concatenate([got_y_ref[1], corner_after], axis=0),
        jnp.concatenate([got_y_ref[0], corner_before], axis=0),
    )
    snow = drift(
        snow, east, north, tile_x, tile_y, gx * tile_x, gy * tile_y,
        tile_x * tiles_x, tile_y * tiles_y, STEPS,
    )
    drift_ref[...] = snow
    exchange = factor_ref[...] / (1.0 + snow)
    tally = tally_ref[...]
    for load in loads[2:]:
        load.wait()
    carry = eliminate(
        temp_ref, rho_ref, size_ref, tally, exchange, air_ref[...], ratio_ref, value_ref
    )

    got_rows(deep_send, deep_got, deep_sems, me, devices, tiles_y)
    high, low, base_diag, base_rhs, flag = deep_places(deep_got[:, 0, 0:LANES], tile_x, tile_y)
    bottom, surface_deep = bottom_row(temp_ref, tally, carry, base_diag, base_rhs, flag)
    answer_send[:, 0, :] = deep_answers(high, low, surface_deep, devices)
    send_rows(answer_send, answer_got, answer_sems, me, devices, tiles_y)

    substitute(value_ref, ratio_ref, value_ref, bottom)
    fresh_out = pltpu.make_async_copy(value_ref, fresh_hbm, out_sems.at[0])
    fresh_out.start()
    runoff = seep(value_ref, rho_ref, fluid_ref, tally, fluid_ref)
    kept_out = pltpu.make_async_copy(fluid_ref, kept_hbm, out_sems.at[1])
    kept_out.start()

    parts = (p0_ref, p1_ref, p2_ref)
    split_three(runoff, parts)
    fill_values(a_ref, high_ref, parts, 2 * rows, tile_x)
    binned = sum(placed_sum(a_ref, code_b_ref, 2 * rows, LANES, columns, 3))
    split_three(binned, parts)
    for half, (holder_ref, b_ref) in enumerate(
        ((own_holder_ref, own_b_ref), (next_holder_ref, next_b_ref))
    ):
        halves = [p.at[pl.ds(half * rows, rows)] for p in parts]
        fill_values(a_ref, holder_ref, halves, devices, rows)
        run_send[:, 0, half * LANES : (half + 1) * LANES] = sum(
            placed_sum(a_ref, b_ref, devices, LANES, reaches, 3)
        )
    send_rows(run_send, run_got, run_sems, me, devices, tiles_y)

    got_rows(answer_send, answer_got, answer_sems, me, devices, tiles_y)
    first = deep_return(answer_got[:, 0, :], owner_col, position, devices)
    deep_substitute(first, elink_ref, dprime_ref, rprime_ref, deep_ref)
    place_ref[...] = deep_got[:, 0, LANES:].astype(jnp.int32)
    got_rows(run_send, run_got, run_sems, me, devices, tiles_y)
    behind = pltpu.roll(run_got[:, 0, LANES:], tiles_y, 0)
    behind = jnp.where(rows_of(behind.shape) >= tiles_y, behind, 0.0)
    total_ref[...] = run_got[:, 0, 0:LANES] + behind

    for halo in halos:
        halo.wait_send()
    for send_ref, got_ref, sems in (
        (deep_send, deep_got, deep_sems),
        (answer_send, answer_got, answer_sems), (run_send, run_got, run_sems),
    ):
        rows_all(send_ref, got_ref, sems, me, devices, tiles_y).wait_send()
    fresh_out.wait()
    kept_out.wait()


def end_kernel(
    pieces, fresh_in, kept_in, drift_in, deep_in, total_ref, place_ref,
    fresh_out, kept_out, drift_out, deep_out, arrival_ref,
    a_ref, b_ref, high_ref, low_ref, p0_ref, p1_ref, p2_ref, sems,
):
    layers = fresh_in.shape[0]
    depth = layers // pieces
    spans = [pl.ds(k * depth, depth) for k in range(pieces)]
    pairs = [(drift_in, drift_out), (deep_in, deep_out)]
    pairs += [(fresh_in.at[span], fresh_out.at[span]) for span in spans]
    pairs += [(kept_in.at[span], kept_out.at[span]) for span in spans]
    copies = [
        pltpu.make_async_copy(source, target, sems.at[k])
        for k, (source, target) in enumerate(pairs)
    ]
    for copy in copies:
        copy.start()
    rows = arrival_ref.shape[0]
    devices = total_ref.shape[0]
    place = place_ref[...]
    high_ref[...] = quotient(place, LANES)
    low_ref[...] = remainder(place, LANES)
    fill_places(b_ref, low_ref, LANES, devices)
    parts = (p0_ref, p1_ref, p2_ref)
    split_three(total_ref[...], parts)
    fill_values(a_ref, high_ref, parts, rows, devices)
    arrival_ref[...] = sum(placed_sum(a_ref, b_ref, rows, LANES, devices * LANES, 3))
    for copy in copies:
        copy.wait()


def local(*args):
    f32, i32, bf16 = jnp.float32, jnp.int32, jnp.bfloat16
    layers, tile_x, tile_y = args[0].shape
    deep_layers, slots = args[10].shape
    tiles_x = lax.axis_size("gx")
    tiles_y = lax.axis_size("gy")
    devices = tiles_x * tiles_y
    columns = tile_x * tile_y
    reaches = args[14].shape[0] // devices
    rows = reaches // LANES
    strata = (layers, tile_x, tile_y)
    deep = (deep_layers, slots)
    edge = 2 * STEPS
    wide = max(3 * 2 * rows, 3 * devices)
    spread = (devices, LANES)
    pieces = 5 if layers % 5 == 0 else 1
    tall = max(tile_x, 2 * rows)
    grid = (rows, LANES)
    message = (devices, 1, LANES)
    scratch = (
        [(strata, f32)] * 4
        + [(grid, i32)] * 2
        + [(strata, f32)] * 2
        + [(deep, f32)] * 3
        + [((2, 3, edge, tile_y), f32), ((tile_x, tile_y), f32), ((2, 3, edge, tile_y), f32)]
        + [((2, tile_x, tile_y), f32), ((4, edge, tile_y), f32)]
        + [((devices, 1, 2 * LANES), f32)] * 2
        + [(message, f32)] * 2
        + [((devices, 1, 2 * LANES), f32)] * 2
        + [((rows * devices, LANES), bf16), ((rows * devices, 2 * LANES), f32)]
        + [(grid, i32)] * 4
        + [((LANES, reaches), bf16)] * 2
        + [((LANES, columns), bf16), ((wide, columns), bf16)]
        + [((tile_x, tile_y), i32)] * 2
        + [((tall, LANES), f32)] * 3
    )
    dma = pltpu.SemaphoreType.DMA
    vmem = pl.BlockSpec(memory_space=pltpu.VMEM)
    anywhere = pl.BlockSpec(memory_space=pl.ANY)
    outs = [((tile_x, tile_y), f32), (strata, f32), (strata, f32), (deep, f32), (spread, f32), (spread, i32)]
    drift_final, fresh, kept, deep_fresh, total, place = pl.pallas_call(
        functools.partial(step_kernel, tiles_x, tiles_y),
        out_shape=[jax.ShapeDtypeStruct(s, d) for s, d in outs],
        in_specs=[anywhere] * 4 + [vmem] * 10 + [anywhere],
        out_specs=[vmem, anywhere, anywhere, vmem, vmem, vmem],
        scratch_shapes=[pltpu.VMEM(s, d) for s, d in scratch]
        + [dma((6,)), dma((2,)), dma((8,)), dma((8,)), dma((2,)), dma((2,)), dma((2,))],
        compiler_params=pltpu.CompilerParams(
            collective_id=0, has_side_effects=True, vmem_limit_bytes=56 * 2**20
        ),
    )(
        args[0], args[1], args[3], args[2], args[4], args[5], args[6], args[7], args[8], args[9],
        args[10], args[11], args[12].reshape(1, slots), args[13],
        args[14].reshape(devices * rows, LANES),
    )
    ends = ((layers, tile_x, tile_y), strata, (tile_x, tile_y), deep, grid)
    fresh, kept, drift_final, deep_fresh, arrival = pl.pallas_call(
        functools.partial(end_kernel, pieces),
        out_shape=[jax.ShapeDtypeStruct(s, f32) for s in ends],
        in_specs=[anywhere] * 4 + [vmem] * 2,
        out_specs=[anywhere] * 4 + [vmem],
        scratch_shapes=[
            pltpu.VMEM((3 * rows, devices * LANES), bf16),
            pltpu.VMEM((LANES, devices * LANES), bf16),
        ]
        + [pltpu.VMEM(spread, i32)] * 2
        + [pltpu.VMEM(spread, f32)] * 3
        + [dma((2 + 2 * pieces,))],
        compiler_params=pltpu.CompilerParams(vmem_limit_bytes=56 * 2**20),
    )(fresh, kept, drift_final, deep_fresh, total, place)
    return drift_final, fresh, kept, deep_fresh, arrival.reshape(reaches)


def solution(mesh):
    cells = P("gx", "gy")
    strata = P(None, "gx", "gy")
    deep = P(None, ("gx", "gy"))
    return jax.shard_map(
        local,
        mesh=mesh,
        in_specs=(strata,) * 4 + (cells,) * 6 + (deep, deep, P(("gx", "gy")), cells, P()),
        out_specs=(cells, strata, strata, deep, P(("gx", "gy"))),
        check_vma=False,
    )
```

```python
import functools

import jax
import jax.numpy as jnp
from jax import lax
from jax.experimental import pallas as pl
from jax.experimental.pallas import tpu as pltpu
from jax.sharding import PartitionSpec as P

STEPS = 4
PAIR = 8
LANES = 128

diffusion_number = 0.1
melt_rate = 0.02
holding_rate = 0.03

HIGH = lax.Precision.HIGHEST
NT = (((1,), (1,)), ((), ()))
TN = (((0,), (0,)), ((), ()))
NN = (((1,), (0,)), ((), ()))


def quotient(x, size):
    if size & (size - 1) == 0:
        return lax.shift_right_logical(x, jnp.full_like(x, size.bit_length() - 1))
    return lax.div(x, jnp.full_like(x, size))


def remainder(x, size):
    if size & (size - 1) == 0:
        return x & (size - 1)
    return lax.rem(x, jnp.full_like(x, size))


def rows_of(shape):
    return lax.broadcasted_iota(jnp.int32, shape, 0)


def lanes_of(shape):
    return lax.broadcasted_iota(jnp.int32, shape, 1)


def dot(a, b, dims, precision=None):
    return lax.dot_general(a, b, dims, precision=precision, preferred_element_type=jnp.float32)


def lane_chunk(i):
    return pl.ds(pl.multiple_of(i * LANES, LANES), LANES)


def fill_places(out_ref, index_ref, places, rows, unroll=4):
    def body(i, carry):
        hit = rows_of((places, LANES)) == index_ref[pl.ds(i, 1), :]
        out_ref[0:places, lane_chunk(i)] = jnp.where(hit, 1.0, 0.0).astype(jnp.bfloat16)
        return carry

    lax.fori_loop(0, rows, body, 0, unroll=unroll)


def fill_values(out_ref, index_ref, part_refs, places, rows, unroll=4):
    def body(i, carry):
        hit = rows_of((places, LANES)) == index_ref[pl.ds(i, 1), :]
        for p, part_ref in enumerate(part_refs):
            out_ref[p * places : (p + 1) * places, lane_chunk(i)] = jnp.where(
                hit, part_ref[pl.ds(i, 1), :], 0.0
            ).astype(jnp.bfloat16)
        return carry

    lax.fori_loop(0, rows, body, 0, unroll=unroll)


def split_three(value, part_refs):
    first = value.astype(jnp.bfloat16).astype(jnp.float32)
    second = (value - first).astype(jnp.bfloat16).astype(jnp.float32)
    rows = value.shape[0]
    part_refs[0][0:rows, :] = first
    part_refs[1][0:rows, :] = second
    part_refs[2][0:rows, :] = value - first - second


def placed_sum(a_ref, b_ref, places, lanes, width, parts):
    both = dot(a_ref[0 : parts * places, 0:width], b_ref[0:lanes, 0:width], NT)
    return [both[p * places : (p + 1) * places] for p in range(parts)]


def deep_eliminate(temp_ref, rho_ref, elink_ref, dprime_ref, rprime_ref):
    layers = temp_ref.shape[0]
    kdeep = 1.0 + 24.0 * rho_ref[...] * rho_ref[...]
    elink_ref[0 : layers - 1, :] = 0.5 * (kdeep[:-1] + kdeep[1:])
    elink_ref[layers - 1 : layers, :] = jnp.zeros_like(kdeep[:1])
    elink = elink_ref[...]
    dprime_ref[...] = 1.0 + elink
    dprime_ref[1:layers, :] = dprime_ref[1:layers, :] + elink[:-1]
    last = pl.ds(layers - 1, 1)
    diag = dprime_ref[last, :] + kdeep[layers - 1 :]
    rhs = temp_ref[last, :]
    dprime_ref[last, :] = diag
    rprime_ref[last, :] = rhs

    def body(step, carry):
        diag, rhs = carry
        row = pl.ds(layers - 2 - step, 1)
        link = elink_ref[row, :]
        ratio = link / diag
        diag = dprime_ref[row, :] - link * ratio
        rhs = temp_ref[row, :] + ratio * rhs
        dprime_ref[row, :] = diag
        rprime_ref[row, :] = rhs
        return diag, rhs

    return lax.fori_loop(0, layers - 1, body, (diag, rhs), unroll=7)


def deep_positions(pile_row, columns):
    slots = pile_row.shape[1]
    pile_col = as_column(pile_row.astype(jnp.float32)).astype(jnp.int32)
    owner_row = quotient(pile_row, columns)
    owner_col = quotient(pile_col, columns)
    square = (slots, slots)
    earlier = (owner_row == owner_col) & (lanes_of(square) < rows_of(square))
    position = jnp.sum(jnp.where(earlier, 1.0, 0.0), axis=1, keepdims=True).astype(jnp.int32)
    return owner_row, owner_col, remainder(pile_col, columns), position


def as_column(row):
    size = row.shape[1]
    eye = rows_of((size, size)) == lanes_of((size, size))
    return jnp.sum(jnp.where(eye, row, 0.0), axis=1, keepdims=True)


def as_row(column):
    size = column.shape[0]
    eye = rows_of((size, size)) == lanes_of((size, size))
    return jnp.sum(jnp.where(eye, column, 0.0), axis=0, keepdims=True)


def deep_message(diag, rhs, owner_row, cell, position, devices):
    slots = owner_row.shape[1]
    lane = lanes_of((slots, LANES))
    cell = (cell + 1).astype(jnp.float32)
    table = jnp.where(lane == position, as_column(diag), 0.0)
    table = jnp.where(lane == position + PAIR, as_column(rhs), table)
    table = jnp.where(lane == position + 2 * PAIR, cell, table)
    pick = jnp.where(rows_of((devices, slots)) == owner_row, 1.0, 0.0)
    return dot(pick, table, NN, HIGH)


def ranks(holder_ref, rank_ref, hit_ref, count_ref, devices, rows):
    def fill(i, carry):
        hit = rows_of((devices, LANES)) == holder_ref[pl.ds(i, 1), :]
        place = pl.ds(pl.multiple_of(i * devices, devices), devices)
        hit_ref[place, :] = jnp.where(hit, 1.0, 0.0).astype(jnp.bfloat16)
        return carry

    lax.fori_loop(0, rows, fill, 0, unroll=4)
    shape = (LANES, 2 * LANES)
    before = (rows_of(shape) < lanes_of(shape)) | (lanes_of(shape) >= LANES)
    count_ref[...] = dot(hit_ref[...], jnp.where(before, 1.0, 0.0).astype(jnp.bfloat16), NN)

    def number(i, base):
        hit = rows_of((devices, LANES)) == holder_ref[pl.ds(i, 1), :]
        place = pl.ds(pl.multiple_of(i * devices, devices), devices)
        count = count_ref[place, 0:LANES] + base
        rank_ref[pl.ds(i, 1), :] = jnp.sum(
            jnp.where(hit, count, 0.0), axis=0, keepdims=True
        ).astype(jnp.int32)
        return base + count_ref[place, LANES : 2 * LANES]

    lax.fori_loop(0, rows, number, jnp.zeros((devices, LANES), jnp.float32), unroll=4)


def drift(snow, east, north, tile_x, tile_y, first_x, first_y, extent_x, extent_y, halo):
    shape = snow.shape
    x = rows_of(shape)
    y = lanes_of(shape)
    x = first_x + jnp.where(x >= tile_x + halo, x - shape[0], x)
    y = first_y + jnp.where(y >= tile_y + halo, y - shape[1], y)
    inside = (x >= 0) & (x < extent_x) & (y >= 0) & (y < extent_y)
    east_up, east_down = jnp.maximum(east, 0.0), jnp.minimum(east, 0.0)
    north_up, north_down = jnp.maximum(north, 0.0), jnp.minimum(north, 0.0)
    snow = jnp.where(inside, snow, 0.0)
    for step in range(STEPS):
        before_x = pltpu.roll(snow, 1, 0)
        after_x = pltpu.roll(snow, shape[0] - 1, 0)
        before_y = pltpu.roll(snow, 1, 1)
        after_y = pltpu.roll(snow, shape[1] - 1, 1)
        change = -east_up * (snow - before_x) - east_down * (after_x - snow)
        change = change - north_up * (snow - before_y) - north_down * (after_y - snow)
        snow = (
            snow
            + change
            + diffusion_number * (before_x + after_x + before_y + after_y - 4.0 * snow)
        )
        snow = jnp.where(inside, snow, 0.0)
    return snow[0:tile_x, 0:tile_y]


def deep_places(got, tile_x, tile_y):
    devices = got.shape[0]
    highs, lows, diags, rhss = [], [], [], []
    for k in range(PAIR):
        cell = got[:, 2 * PAIR + k : 2 * PAIR + k + 1].astype(jnp.int32) - 1
        full = cell >= 0
        cell = jnp.maximum(cell, 0)
        high = (lanes_of((devices, tile_x)) == quotient(cell, tile_y)) & full
        low = (lanes_of((devices, tile_y)) == remainder(cell, tile_y)) & full
        highs.append(jnp.where(high, 1.0, 0.0))
        low = jnp.where(low, 1.0, 0.0)
        lows.append(low)
        diags.append(low * got[:, k : k + 1])
        rhss.append(low * got[:, PAIR + k : PAIR + k + 1])
    high = jnp.concatenate(highs, axis=0)
    low = jnp.concatenate(lows, axis=0)
    table = jnp.concatenate(
        [jnp.concatenate(diags, axis=0), jnp.concatenate(rhss, axis=0), low], axis=1
    )
    dense = dot(high, table, TN, HIGH)
    return (
        high,
        low,
        dense[:, 0:tile_y],
        dense[:, tile_y : 2 * tile_y],
        dense[:, 2 * tile_y :],
    )


def deep_answers(high, low, dense, devices):
    found = dot(high, dense, NN, HIGH) * low
    lane = lanes_of((devices, LANES))
    answer = jnp.zeros((devices, LANES), jnp.float32)
    for k in range(PAIR):
        value = jnp.sum(found[k * devices : (k + 1) * devices], axis=1, keepdims=True)
        answer = jnp.where(lane == k, value, answer)
    return answer


def eliminate(temp_ref, rho_ref, size_ref, tally, exchange, air, ratio_ref, value_ref):
    layers = temp_ref.shape[0]

    def kappa_of(i):
        rho = rho_ref[i]
        return 1.0 + 24.0 * rho * rho * size_ref[i]

    def row(i, kappa, up, ratio, value, diag_more, rhs_more):
        kappa_next = kappa_of(i + 1)
        down = jnp.where(i + 1 < tally, 0.5 * (kappa + kappa_next), 0.0)
        diag = 1.0 + up + down + jnp.where(i == tally - 1, kappa, 0.0)
        rhs = temp_ref[i]
        if diag_more is not None:
            diag = diag + diag_more
            rhs = rhs + rhs_more
        inverse = 1.0 / (diag - up * ratio)
        value = (rhs + up * value) * inverse
        ratio = down * inverse
        ratio_ref[i] = ratio
        value_ref[i] = value
        return kappa_next, down, ratio, value

    zero = jnp.zeros_like(air)
    carry = row(0, kappa_of(0), zero, zero, zero, exchange, exchange * air)
    return lax.fori_loop(
        1, layers - 1, lambda i, c: row(i, *c, None, None), carry, unroll=2
    )


def bottom_row(temp_ref, tally, carry, base_diag, base_rhs, flag):
    layers = temp_ref.shape[0]
    kappa, up, ratio, value = carry
    scale = flag * kappa / (base_diag + kappa)
    diag = 1.0 + up + jnp.where(tally == layers, kappa, 0.0) - scale * kappa
    rhs = temp_ref[layers - 1] + scale * base_rhs
    bottom = (rhs + up * value) / (diag - up * ratio)
    surface_deep = (base_rhs + kappa * bottom) / (base_diag + kappa)
    return bottom, surface_deep


def substitute(fresh_ref, ratio_ref, value_ref, bottom):
    layers = fresh_ref.shape[0]
    fresh_ref[layers - 1] = bottom

    def body(step, below):
        i = layers - 2 - step
        below = value_ref[i] + ratio_ref[i] * below
        fresh_ref[i] = below
        return below

    lax.fori_loop(0, layers - 1, body, bottom, unroll=7)


def seep(fresh_ref, rho_ref, fluid_ref, tally, kept_ref):
    layers = fresh_ref.shape[0]

    def body(i, flux):
        live = i < tally
        source = fluid_ref[i] + melt_rate * jnp.maximum(fresh_ref[i], 0.0)
        avail = jnp.where(live, source, 0.0) + flux
        kept = jnp.where(live, jnp.minimum(avail, holding_rate * (1.0 - rho_ref[i])), 0.0)
        kept_ref[i] = kept
        return avail - kept

    return lax.fori_loop(0, layers, body, jnp.zeros(tally.shape, jnp.float32), unroll=5)


def deep_return(returned, owner_col, position, devices):
    slots = position.shape[0]
    pick = jnp.where(lanes_of((slots, devices)) == owner_col, 1.0, 0.0)
    found = dot(pick, returned, NN, HIGH)
    lane = lanes_of((slots, LANES))
    return as_row(jnp.sum(jnp.where(lane == position, found, 0.0), axis=1, keepdims=True))


def deep_substitute(first, elink_ref, dprime_ref, rprime_ref, out_ref):
    layers = out_ref.shape[0]
    inverse = 1.0 / dprime_ref[...]
    rprime_ref[...] = rprime_ref[...] * inverse
    dprime_ref[1:layers, :] = elink_ref[0 : layers - 1, :] * inverse[1:]
    out_ref[0:1, :] = first

    def body(j, above):
        row = pl.ds(j, 1)
        above = rprime_ref[row, :] + dprime_ref[row, :] * above
        out_ref[row, :] = above
        return above

    lax.fori_loop(1, layers, body, first, unroll=7)


def peer_id(peer, tiles_y):
    return {"gx": lax.div(peer, tiles_y), "gy": lax.rem(peer, tiles_y)}


def row_copy(send_ref, got_ref, sems, source, target, device, tiles_y):
    return pltpu.make_async_remote_copy(
        src_ref=send_ref.at[source],
        dst_ref=got_ref.at[target],
        send_sem=sems.at[0],
        recv_sem=sems.at[1],
        device_id=peer_id(device, tiles_y),
        device_id_type=pl.DeviceIdType.MESH,
    )


def send_rows(send_ref, got_ref, sems, me, devices, tiles_y):
    def body(step, carry):
        peer = lax.rem(me + step, devices)
        row_copy(send_ref, got_ref, sems, peer, me, peer, tiles_y).start()
        return carry

    lax.fori_loop(1, devices, body, 0, unroll=4)


def rows_all(send_ref, got_ref, sems, me, devices, tiles_y):
    every = pl.ds(0, devices - 1)
    return row_copy(send_ref, got_ref, sems, every, every, lax.rem(me + 1, devices), tiles_y)


def got_rows(send_ref, got_ref, sems, me, devices, tiles_y):
    rows_all(send_ref, got_ref, sems, me, devices, tiles_y).wait_recv()
    got_ref[pl.ds(me, 1)] = send_ref[pl.ds(me, 1)]


def pack_sides(fields, strip_ref):
    shape = fields[0].shape
    lane = lanes_of(shape)
    packed = jnp.zeros(shape, jnp.float32)
    for f, field in enumerate(fields):
        first = 4 * f
        last = 16 + 4 * f
        moved = pltpu.roll(field, first, 1) if first else field
        packed = jnp.where((lane >= first) & (lane < first + STEPS), moved, packed)
        moved = pltpu.roll(field, STEPS + last, 1)
        packed = jnp.where((lane >= last) & (lane < last + STEPS), moved, packed)
    strip_ref[...] = packed


def joined_fields(fields, before_x, after_x, sides_after, sides_before):
    lane = lanes_of(sides_after.shape)
    out = []
    for f, field in enumerate(fields):
        ends = jnp.where(rows_of(after_x[f].shape) < STEPS, after_x[f], before_x[f])
        core = jnp.concatenate([field, ends], axis=0)
        first = 4 * f
        last = 16 + 4 * f
        after_y = pltpu.roll(sides_after, LANES - first, 1) if first else sides_after
        before_y = pltpu.roll(sides_before, LANES - STEPS - last, 1)
        side = jnp.where(lane < STEPS, after_y, jnp.where(lane >= LANES - STEPS, before_y, 0.0))
        out.append(jnp.concatenate([core, side], axis=1))
    return out


def step_kernel(
    tiles_x, tiles_y,
    temp_hbm, rho_hbm, size_hbm, fluid_hbm, tally_ref, air_ref, factor_ref, snow_ref, east_ref,
    north_ref, deep_temp_ref, deep_rho_ref, pile_ref, code_ref, index_hbm,
    drift_ref, fresh_hbm, kept_hbm, deep_ref, total_ref, place_ref,
    temp_ref, rho_ref, size_ref, fluid_ref, own_ref, next_ref, ratio_ref, value_ref,
    elink_ref, dprime_ref, rprime_ref, strip_x_ref, strip_y_ref, got_x_ref, got_y_ref, got_d_ref,
    deep_send, deep_got, answer_send, answer_got, run_send, run_got,
    hit_ref, count_ref, own_rank_ref, next_rank_ref, own_holder_ref, next_holder_ref,
    own_b_ref, next_b_ref, code_b_ref, a_ref, high_ref, low_ref, p0_ref, p1_ref, p2_ref, in_sems, out_sems, halo_send, halo_got, deep_sems,
    answer_sems, run_sems,
):
    devices = tiles_x * tiles_y
    tile_x, tile_y = tally_ref.shape
    columns = tile_x * tile_y
    rows = own_ref.shape[0]
    reaches = rows * LANES
    gx, gy = lax.axis_index("gx"), lax.axis_index("gy")
    me = gx * tiles_y + gy
    follow = jnp.minimum(gx + 1, tiles_x - 1) * tiles_y + gy

    barrier = pltpu.get_barrier_semaphore()

    def greet(step, carry):
        pl.semaphore_signal(
            barrier, inc=1, device_id=peer_id(lax.rem(me + step, devices), tiles_y),
            device_id_type=pl.DeviceIdType.MESH,
        )
        return carry

    lax.fori_loop(1, devices, greet, 0)
    loads = [
        pltpu.make_async_copy(source, target, in_sems.at[k])
        for k, (source, target) in enumerate(
            (
                (index_hbm.at[pl.ds(pl.multiple_of(me * rows, 8), rows)], own_ref),
                (index_hbm.at[pl.ds(pl.multiple_of(follow * rows, 8), rows)], next_ref),
                (temp_hbm, temp_ref),
                (rho_hbm, rho_ref),
                (size_hbm, size_ref),
                (fluid_hbm, fluid_ref),
            )
        )
    ]
    for load in loads:
        load.start()

    edge = 2 * STEPS
    fields = (snow_ref[...], east_ref[...], north_ref[...])
    for f, field in enumerate(fields):
        strip_x_ref[0, f] = field[0:edge]
        strip_x_ref[1, f] = field[tile_x - edge : tile_x]
    pack_sides(fields, strip_y_ref)
    diag, rhs = deep_eliminate(deep_temp_ref, deep_rho_ref, elink_ref, dprime_ref, rprime_ref)
    owner_row, owner_col, cell, position = deep_positions(pile_ref[...], columns)
    deep_send[:, 0, 0:LANES] = deep_message(diag, rhs, owner_row, cell, position, devices)

    pl.semaphore_wait(barrier, devices - 1)
    up_x, down_x = lax.rem(gx + 1, tiles_x), lax.rem(gx + tiles_x - 1, tiles_x)
    up_y, down_y = lax.rem(gy + 1, tiles_y), lax.rem(gy + tiles_y - 1, tiles_y)
    head = strip_y_ref.at[pl.ds(0, edge)]
    tail = strip_y_ref.at[pl.ds(tile_x - edge, edge)]
    halos = [
        pltpu.make_async_remote_copy(
            src_ref=source, dst_ref=target, send_sem=halo_send.at[k], recv_sem=halo_got.at[k],
            device_id={"gx": x, "gy": y}, device_id_type=pl.DeviceIdType.MESH,
        )
        for k, (source, target, x, y) in enumerate(
            (
                (strip_x_ref.at[1], got_x_ref.at[0], up_x, gy),
                (strip_x_ref.at[0], got_x_ref.at[1], down_x, gy),
                (strip_y_ref, got_y_ref.at[0], gx, up_y),
                (strip_y_ref, got_y_ref.at[1], gx, down_y),
                (tail, got_d_ref.at[0], up_x, up_y),
                (tail, got_d_ref.at[1], up_x, down_y),
                (head, got_d_ref.at[2], down_x, up_y),
                (head, got_d_ref.at[3], down_x, down_y),
            )
        )
    ]
    for halo in halos:
        halo.start()

    loads[0].wait()
    loads[1].wait()
    own_holder_ref[...] = quotient(own_ref[...], reaches)
    next_holder_ref[...] = quotient(next_ref[...], reaches)
    ranks(own_holder_ref, own_rank_ref, hit_ref, count_ref, devices, rows)
    fill_places(own_b_ref, own_rank_ref, LANES, rows)
    spot = remainder(own_ref[...], reaches)
    p0_ref[0:rows, :] = quotient(spot, LANES).astype(jnp.float32)
    p1_ref[0:rows, :] = remainder(spot, LANES).astype(jnp.float32)
    fill_values(a_ref, own_holder_ref, (p0_ref, p1_ref), devices, rows)
    high, low = placed_sum(a_ref, own_b_ref, devices, LANES, reaches, 2)
    deep_send[:, 0, LANES:] = high * LANES + low
    send_rows(deep_send, deep_got, deep_sems, me, devices, tiles_y)
    ranks(next_holder_ref, next_rank_ref, hit_ref, count_ref, devices, rows)
    fill_places(next_b_ref, next_rank_ref, LANES, rows)
    high_ref[...] = quotient(code_ref[...], LANES)
    low_ref[...] = remainder(code_ref[...], LANES)
    fill_places(code_b_ref, low_ref, LANES, tile_x)

    for halo in halos:
        halo.wait_recv()
    near = rows_of((edge, LANES)) < STEPS
    corner_after = jnp.where(near, got_d_ref[3], got_d_ref[1])
    corner_before = jnp.where(near, got_d_ref[2], got_d_ref[0])
    snow, east, north = joined_fields(
        fields,
        [got_x_ref[0, f] for f in range(3)],
        [got_x_ref[1, f] for f in range(3)],
        jnp.concatenate([got_y_ref[1], corner_after], axis=0),
        jnp.concatenate([got_y_ref[0], corner_before], axis=0),
    )
    snow = drift(
        snow, east, north, tile_x, tile_y, gx * tile_x, gy * tile_y,
        tile_x * tiles_x, tile_y * tiles_y, STEPS,
    )
    drift_ref[...] = snow
    exchange = factor_ref[...] / (1.0 + snow)
    tally = tally_ref[...]
    for load in loads[2:]:
        load.wait()
    carry = eliminate(
        temp_ref, rho_ref, size_ref, tally, exchange, air_ref[...], ratio_ref, value_ref
    )

    got_rows(deep_send, deep_got, deep_sems, me, devices, tiles_y)
    high, low, base_diag, base_rhs, flag = deep_places(deep_got[:, 0, 0:LANES], tile_x, tile_y)
    bottom, surface_deep = bottom_row(temp_ref, tally, carry, base_diag, base_rhs, flag)
    answer_send[:, 0, :] = deep_answers(high, low, surface_deep, devices)
    send_rows(answer_send, answer_got, answer_sems, me, devices, tiles_y)

    substitute(value_ref, ratio_ref, value_ref, bottom)
    fresh_out = pltpu.make_async_copy(value_ref, fresh_hbm, out_sems.at[0])
    fresh_out.start()
    runoff = seep(value_ref, rho_ref, fluid_ref, tally, fluid_ref)
    kept_out = pltpu.make_async_copy(fluid_ref, kept_hbm, out_sems.at[1])
    kept_out.start()

    parts = (p0_ref, p1_ref, p2_ref)
    split_three(runoff, parts)
    fill_values(a_ref, high_ref, parts, 2 * rows, tile_x)
    binned = sum(placed_sum(a_ref, code_b_ref, 2 * rows, LANES, columns, 3))
    split_three(binned, parts)
    for half, (holder_ref, b_ref) in enumerate(
        ((own_holder_ref, own_b_ref), (next_holder_ref, next_b_ref))
    ):
        halves = [p.at[pl.ds(half * rows, rows)] for p in parts]
        fill_values(a_ref, holder_ref, halves, devices, rows)
        run_send[:, 0, half * LANES : (half + 1) * LANES] = sum(
            placed_sum(a_ref, b_ref, devices, LANES, reaches, 3)
        )
    send_rows(run_send, run_got, run_sems, me, devices, tiles_y)

    got_rows(answer_send, answer_got, answer_sems, me, devices, tiles_y)
    first = deep_return(answer_got[:, 0, :], owner_col, position, devices)
    deep_substitute(first, elink_ref, dprime_ref, rprime_ref, deep_ref)
    place_ref[...] = deep_got[:, 0, LANES:].astype(jnp.int32)
    got_rows(run_send, run_got, run_sems, me, devices, tiles_y)
    behind = pltpu.roll(run_got[:, 0, LANES:], tiles_y, 0)
    behind = jnp.where(rows_of(behind.shape) >= tiles_y, behind, 0.0)
    total_ref[...] = run_got[:, 0, 0:LANES] + behind

    for halo in halos:
        halo.wait_send()
    for send_ref, got_ref, sems in (
        (deep_send, deep_got, deep_sems),
        (answer_send, answer_got, answer_sems), (run_send, run_got, run_sems),
    ):
        rows_all(send_ref, got_ref, sems, me, devices, tiles_y).wait_send()
    fresh_out.wait()
    kept_out.wait()


def end_kernel(
    pieces, fresh_in, kept_in, drift_in, deep_in, total_ref, place_ref,
    fresh_out, kept_out, drift_out, deep_out, arrival_ref,
    a_ref, b_ref, high_ref, low_ref, p0_ref, p1_ref, p2_ref,
    fresh_ref, kept_ref, drift_ref, deep_ref, in_sems, out_sems,
):
    layers = fresh_in.shape[0]
    depth = layers // pieces
    spans = [pl.ds(k * depth, depth) for k in range(pieces)]
    trips = [(drift_in, drift_ref, drift_out), (deep_in, deep_ref, deep_out)]
    for span in spans:
        trips.append((fresh_in.at[span], fresh_ref.at[span], fresh_out.at[span]))
        trips.append((kept_in.at[span], kept_ref.at[span], kept_out.at[span]))
    inward = [
        pltpu.make_async_copy(source, stop, in_sems.at[k])
        for k, (source, stop, target) in enumerate(trips)
    ]
    outward = [
        pltpu.make_async_copy(stop, target, out_sems.at[k])
        for k, (source, stop, target) in enumerate(trips)
    ]
    for copy in inward:
        copy.start()
    rows = arrival_ref.shape[0]
    devices = total_ref.shape[0]
    place = place_ref[...]
    high_ref[...] = quotient(place, LANES)
    low_ref[...] = remainder(place, LANES)
    fill_places(b_ref, low_ref, LANES, devices)
    for arrived, copy in zip(inward, outward):
        arrived.wait()
        copy.start()
    parts = (p0_ref, p1_ref, p2_ref)
    split_three(total_ref[...], parts)
    fill_values(a_ref, high_ref, parts, rows, devices)
    arrival_ref[...] = sum(placed_sum(a_ref, b_ref, rows, LANES, devices * LANES, 3))
    for copy in outward:
        copy.wait()


def local(*args):
    f32, i32, bf16 = jnp.float32, jnp.int32, jnp.bfloat16
    layers, tile_x, tile_y = args[0].shape
    deep_layers, slots = args[10].shape
    tiles_x = lax.axis_size("gx")
    tiles_y = lax.axis_size("gy")
    devices = tiles_x * tiles_y
    columns = tile_x * tile_y
    reaches = args[14].shape[0] // devices
    rows = reaches // LANES
    strata = (layers, tile_x, tile_y)
    deep = (deep_layers, slots)
    edge = 2 * STEPS
    wide = max(3 * 2 * rows, 3 * devices)
    spread = (devices, LANES)
    pieces = 5 if layers % 5 == 0 else 1
    tall = max(tile_x, 2 * rows)
    grid = (rows, LANES)
    message = (devices, 1, LANES)
    scratch = (
        [(strata, f32)] * 4
        + [(grid, i32)] * 2
        + [(strata, f32)] * 2
        + [(deep, f32)] * 3
        + [((2, 3, edge, tile_y), f32), ((tile_x, tile_y), f32), ((2, 3, edge, tile_y), f32)]
        + [((2, tile_x, tile_y), f32), ((4, edge, tile_y), f32)]
        + [((devices, 1, 2 * LANES), f32)] * 2
        + [(message, f32)] * 2
        + [((devices, 1, 2 * LANES), f32)] * 2
        + [((rows * devices, LANES), bf16), ((rows * devices, 2 * LANES), f32)]
        + [(grid, i32)] * 4
        + [((LANES, reaches), bf16)] * 2
        + [((LANES, columns), bf16), ((wide, columns), bf16)]
        + [((tile_x, tile_y), i32)] * 2
        + [((tall, LANES), f32)] * 3
    )
    dma = pltpu.SemaphoreType.DMA
    vmem = pl.BlockSpec(memory_space=pltpu.VMEM)
    anywhere = pl.BlockSpec(memory_space=pl.ANY)
    outs = [((tile_x, tile_y), f32), (strata, f32), (strata, f32), (deep, f32), (spread, f32), (spread, i32)]
    drift_final, fresh, kept, deep_fresh, total, place = pl.pallas_call(
        functools.partial(step_kernel, tiles_x, tiles_y),
        out_shape=[jax.ShapeDtypeStruct(s, d) for s, d in outs],
        in_specs=[anywhere] * 4 + [vmem] * 10 + [anywhere],
        out_specs=[vmem, anywhere, anywhere, vmem, vmem, vmem],
        scratch_shapes=[pltpu.VMEM(s, d) for s, d in scratch]
        + [dma((6,)), dma((2,)), dma((8,)), dma((8,)), dma((2,)), dma((2,)), dma((2,))],
        compiler_params=pltpu.CompilerParams(
            collective_id=0, has_side_effects=True, vmem_limit_bytes=56 * 2**20
        ),
    )(
        args[0], args[1], args[3], args[2], args[4], args[5], args[6], args[7], args[8], args[9],
        args[10], args[11], args[12].reshape(1, slots), args[13],
        args[14].reshape(devices * rows, LANES),
    )
    ends = ((layers, tile_x, tile_y), strata, (tile_x, tile_y), deep, grid)
    fresh, kept, drift_final, deep_fresh, arrival = pl.pallas_call(
        functools.partial(end_kernel, pieces),
        out_shape=[jax.ShapeDtypeStruct(s, f32) for s in ends],
        in_specs=[anywhere] * 4 + [vmem] * 2,
        out_specs=[anywhere] * 4 + [vmem],
        scratch_shapes=[
            pltpu.VMEM((3 * rows, devices * LANES), bf16),
            pltpu.VMEM((LANES, devices * LANES), bf16),
        ]
        + [pltpu.VMEM(spread, i32)] * 2
        + [pltpu.VMEM(spread, f32)] * 3
        + [pltpu.VMEM(s, f32) for s in (strata, strata, (tile_x, tile_y), deep)]
        + [dma((2 + 2 * pieces,))] * 2,
        compiler_params=pltpu.CompilerParams(vmem_limit_bytes=56 * 2**20),
    )(fresh, kept, drift_final, deep_fresh, total, place)
    return drift_final, fresh, kept, deep_fresh, arrival.reshape(reaches)


def solution(mesh):
    cells = P("gx", "gy")
    strata = P(None, "gx", "gy")
    deep = P(None, ("gx", "gy"))
    return jax.shard_map(
        local,
        mesh=mesh,
        in_specs=(strata,) * 4 + (cells,) * 6 + (deep, deep, P(("gx", "gy")), cells, P()),
        out_specs=(cells, strata, strata, deep, P(("gx", "gy"))),
        check_vma=False,
    )
```
